256 devices in a mesh: clus: 64 (over z, x, core), rep: 4 (over y).
Axes of the slice: x: 4, y: 4, z: 8, core: 2. Of those that a mesh axis runs over, the one named last changes fastest.
Arguments:
- density: bfloat16 [1024, 8, 256], P('clus'), may hold values from -6 to 6
- positions: bfloat16 [1024, 3, 256], P('clus'), may hold values from 0 to 1
- areas: bfloat16 [1024, 256], P('clus'), may hold values from 0.29882812 to 3
- near_pairs: int32 [64, 4, 64, 4, 2], P('clus', 'rep'), may hold values from 0 to 1023, as said below
- near_counts: int32 [64, 4, 64], P('clus', 'rep'), may hold values from 1 to 4, as said below
- far_pairs: int32 [64, 4, 64, 2, 2], P('clus', 'rep'), may hold values from 0 to 1023, as said below
- far_counts: int32 [64, 4, 64], P('clus', 'rep'), may hold values from 1 to 2
- far_right: bfloat16 [64, 4, 64, 2, 32, 256], P('clus', 'rep'), may hold values from -0.375 to 0.375
- far_left: bfloat16 [64, 4, 64, 2, 32, 256], P('clus', 'rep'), may hold values from -0.125 to 0.125
Outputs:
- potential: float32 [1024, 8, 256], P('clus')
The draws below stay inside these ranges and needn't reach their ends.
Inputs may be any that keep to these rules, and one draw needn't show every extreme that they name: `near_pairs`: slot [d, u, e, k] holds a pair (i, j) with i owned by index d of clus and j by index e, where cluster c is owned by index c // 16; i != j; pairs may repeat; slots that are not live hold valid pairs too. `near_counts`: equal to 4 where owner e is within two indices of d along clus, counted around the axis. `far_pairs`: slot [d, u, e, k] holds a pair (i, j) with i owned by index d of clus and j by index e, where cluster c is owned by index c // 16; i != j; its factors stand at the same slot of far_right and far_left; slots that are not live hold valid pairs too.
All inputs are finite; a program needn't handle non-finite values.
Results may differ from the reference program's by a relative error of at most 0.0029.
Values may be sent and summed in bfloat16 or wider, within the bound.
A program may use at most 128 MiB of HBM per device.

```python
import math
import jax
import jax.numpy as jnp
from jax import lax

S = 256
DIRS = 8
RANK = 32
CL_DEV = 16
CAPN = 4
CAPF = 2
CLUSTERS = 1024
N_CLUS = 64
N_REP = 4


def pair_draw(key, slots):
    key_rows, key_cols = jax.random.split(key)
    grid_shape = (N_CLUS, N_REP, N_CLUS, slots)
    local_rows = jax.random.randint(key_rows, grid_shape, 0, CL_DEV)
    local_cols = jax.random.randint(key_cols, grid_shape, 0, CL_DEV)
    local_rows = local_rows.at[0, 0, 0, 0].set(0).at[-1, 0, -1, 0].set(CL_DEV - 1)
    local_cols = local_cols.at[0, 0, 0, 0].set(1).at[-1, 0, -1, 0].set(CL_DEV - 2)
    sources = jnp.arange(N_CLUS, dtype=jnp.int32).reshape(-1, 1, 1, 1)
    targets = jnp.arange(N_CLUS, dtype=jnp.int32).reshape(1, 1, -1, 1)
    clash = (sources == targets) & (local_rows == local_cols)
    local_cols = jnp.where(clash, (local_cols + 1) % CL_DEV, local_cols)
    return jnp.stack([sources * CL_DEV + local_rows, targets * CL_DEV + local_cols], axis=-1).astype(jnp.int32)


def draw_near_pairs(key, part):
    key = jax.random.fold_in(key, 11)
    return pair_draw(key, CAPN)


def draw_far_pairs(key, part):
    key = jax.random.fold_in(key, 23)
    return pair_draw(key, CAPF)


def draw_near_counts(key, part):
    key = jax.random.fold_in(key, 31)
    key_heavy, key_count = jax.random.split(key)
    heavy = jax.random.randint(key_heavy, (N_CLUS, 1, 1), 0, 2)
    heavy = heavy.at[0, 0, 0].set(1).at[1, 0, 0].set(0)
    distant = jax.random.randint(key_count, (N_CLUS, N_REP, N_CLUS), CAPN - 1, CAPN + 1)
    distant = jnp.where(heavy == 1, distant, 1)
    sources = jnp.arange(N_CLUS, dtype=jnp.int32).reshape(-1, 1, 1)
    targets = jnp.arange(N_CLUS, dtype=jnp.int32).reshape(1, 1, -1)
    apart = jnp.minimum((targets - sources) % N_CLUS, (sources - targets) % N_CLUS)
    return jnp.where(apart <= 2, CAPN, distant).astype(jnp.int32)


def draw_far_counts(key, part):
    key = jax.random.fold_in(key, 37)
    counts = jax.random.randint(key, (N_CLUS, N_REP, N_CLUS), 1, CAPF + 1)
    return counts.at[0, 0, 0].set(CAPF).astype(jnp.int32)


def block_scale(key, extent, cuts, low, high):
    def one(dim, blocks):
        draws = jax.random.uniform(jax.random.fold_in(jax.random.fold_in(key, 6), dim), (blocks,), jnp.float32, low / len(cuts), high / len(cuts))
        return jnp.repeat(jnp.exp(draws), extent[dim] // blocks).reshape((-1,) + (1,) * (len(extent) - dim - 1))

    loudness = one(*cuts[0])
    for cut in cuts[1:]:
        loudness = loudness * one(*cut)
    return loudness


def scatter_about(key, extent, scale, most, shards=(), kind=jnp.bfloat16):
    values = jax.random.normal(key, extent, jnp.float32) * scale
    if len(shards) > 0:
        values = block_scale(key, extent, shards, -0.22, 0.18) * values
    return jnp.clip(values, min=-most, max=most).astype(kind)


def setup_inputs(seed: int = 0) -> dict:
    key_of = jax.random.split(jax.random.key(seed), 10)
    return {
        "density": scatter_about(key_of[0], (CLUSTERS, DIRS, S), 1.0, 6.0, ((0, 64),)),
        "positions": jnp.clip(1.0 * jax.random.uniform(key_of[1], (CLUSTERS, 3, S), jnp.float32) ** block_scale(key_of[1], (CLUSTERS, 3, S), ((0, 64),), -0.2, 0.2), 0.0, 1.0).astype(jnp.bfloat16),
        "areas": jnp.clip(jnp.exp(math.log(3.0) - 2.306499 * jax.random.uniform(key_of[2], (CLUSTERS, S), jnp.float32) ** block_scale(key_of[2], (CLUSTERS, S), ((0, 64),), -0.2, 0.2)), 0.29882812, 3.0).astype(jnp.bfloat16),
        "near_pairs": draw_near_pairs(jax.random.fold_in(key_of[9], 71), 0),
        "near_counts": draw_near_counts(jax.random.fold_in(key_of[9], 71), 0),
        "far_pairs": draw_far_pairs(jax.random.fold_in(key_of[9], 71), 0),
        "far_counts": draw_far_counts(jax.random.fold_in(key_of[9], 71), 0),
        "far_right": scatter_about(key_of[7], (N_CLUS, N_REP, N_CLUS, CAPF, RANK, S), S ** -0.5, 0.375, ((0, 64), (1, 4))),
        "far_left": scatter_about(key_of[8], (N_CLUS, N_REP, N_CLUS, CAPF, RANK, S), (64 * RANK) ** -0.5, 0.125, ((0, 64), (1, 4))),
    }


softening = 0.01

def rounded(values):
    return lax.optimization_barrier(values.astype(jnp.bfloat16)).astype(jnp.float32)

def build(left_pos, left_area, right_pos, right_area):
    left_pos = left_pos.astype(jnp.float32)
    right_pos = right_pos.astype(jnp.float32)
    squared = (left_pos[..., 0, :, None] - right_pos[..., 0, None, :]) ** 2
    squared = squared + (left_pos[..., 1, :, None] - right_pos[..., 1, None, :]) ** 2
    squared = squared + (left_pos[..., 2, :, None] - right_pos[..., 2, None, :]) ** 2
    weight_pair = left_area.astype(jnp.float32)[..., :, None] * right_area.astype(jnp.float32)[..., None, :]
    return weight_pair / (S * jnp.sqrt(squared + softening))

def live_table(counts, slots):
    table = jnp.arange(slots, dtype=jnp.int32)[None, None, None, :] < counts[..., None]
    return table.astype(jnp.float32).reshape(N_CLUS * N_REP, N_CLUS * slots)

def reference(density, positions, areas, near_pairs, near_counts, far_pairs, far_counts, far_right, far_left):
    high_precision = lax.Precision.HIGHEST
    potential = jnp.zeros((CLUSTERS, DIRS, S), jnp.float32)
    near_list = near_pairs.reshape(N_CLUS * N_REP, N_CLUS * CAPN, 2)
    near_live = live_table(near_counts, CAPN)

    def near_step(running, pieces):
        pair_ids, live = pieces
        row_ids = pair_ids[:, 0]
        column_indices = pair_ids[:, 1]
        tile_set = rounded(build(positions[row_ids], areas[row_ids], positions[column_indices], areas[column_indices]))
        row_contributions = jnp.einsum('tab,trb->tra', tile_set, density[column_indices].astype(jnp.float32), precision=high_precision)
        col_terms = jnp.einsum('tab,tra->trb', tile_set, density[row_ids].astype(jnp.float32), precision=high_precision)
        row_contributions = row_contributions * live[:, None, None]
        col_terms = col_terms * live[:, None, None]
        return (running.at[row_ids].add(row_contributions).at[column_indices].add(col_terms), None)
    potential, _ = lax.scan(near_step, potential, (near_list, near_live))
    far_list = far_pairs.reshape(N_CLUS * N_REP, N_CLUS * CAPF, 2)
    far_live = live_table(far_counts, CAPF)
    right_all = far_right.reshape(N_CLUS * N_REP, N_CLUS * CAPF, RANK, S)
    left_all = far_left.reshape(N_CLUS * N_REP, N_CLUS * CAPF, RANK, S)

    def far_step(running, pieces):
        pair_ids, live, right_f, left_f = pieces
        row_ids = pair_ids[:, 0]
        column_indices = pair_ids[:, 1]
        right_f = right_f.astype(jnp.float32)
        left_f = left_f.astype(jnp.float32)
        projected_col = rounded(jnp.einsum('tqs,trs->tqr', right_f, density[column_indices].astype(jnp.float32), precision=high_precision))
        projected_row = rounded(jnp.einsum('tqs,trs->tqr', left_f, density[row_ids].astype(jnp.float32), precision=high_precision))
        row_contributions = jnp.einsum('tqr,tqs->trs', projected_col, left_f, precision=high_precision) * live[:, None, None]
        col_terms = jnp.einsum('tqr,tqs->trs', projected_row, right_f, precision=high_precision) * live[:, None, None]
        return (running.at[row_ids].add(row_contributions).at[column_indices].add(col_terms), None)
    potential, _ = lax.scan(far_step, potential, (far_list, far_live, right_all, left_all))
    owned_ids = jnp.arange(CLUSTERS, dtype=jnp.int32).reshape(N_CLUS, CL_DEV)

    def self_step(running, group):
        tile_set = rounded(build(positions[group], areas[group], positions[group], areas[group]))
        self_terms = jnp.einsum('tab,trb->tra', tile_set, density[group].astype(jnp.float32), precision=high_precision)
        return (running.at[group].add(self_terms), None)
    potential, _ = lax.scan(self_step, potential, owned_ids)
    return potential
```

```python
import functools

import jax
import jax.numpy as jnp
from jax import lax
from jax.experimental import pallas as pl
from jax.experimental.pallas import tpu as pltpu
from jax.sharding import Mesh, PartitionSpec as P

f32=jnp.float32; bf16=jnp.bfloat16
NA=128; NB=32; NSELF=4; NBT=37
KF=48
G=16

def split3(v):
    h = v.astype(bf16).astype(f32)
    m = (v-h).astype(bf16).astype(f32)
    l = (v-h-m).astype(bf16).astype(f32)
    return h,m,l

def feats(pack_ref, b, vref, left):
    X=[pack_ref[b,128+16*k:144+16*k,:].astype(f32)-0.5 for k in range(3)]
    a=pack_ref[b,176:192,:].astype(f32)
    w=256.0/(a*a)
    n=(X[0]*X[0]+X[1]*X[1]+X[2]*X[2]+0.005)*w
    s=-2.0 if left else 1.0
    rows=[n,w] if left else [w,n]
    rows+= [X[k]*(s*w) for k in range(3)]
    for k,r in enumerate(rows):
        vref[0,pl.ds(k,16,stride=8),:]=r[:,:128]
        vref[1,pl.ds(k,16,stride=8),:]=r[:,128:]

def row8(vref,o):
    return jnp.concatenate([vref[0,pl.ds(o,8),:],vref[1,pl.ds(o,8),:]],1)

def near_kernel(info, pa_ref, pb_ref, own_ref, acca_ref, accb_ref, vl, lf, rt, da, db, sa, sb, ub, ii, jj):
    own = lax.axis_index("x")*2+lax.axis_index("c")
    y = lax.axis_index("y")
    vl[...]=jnp.zeros_like(vl)
    def prep_a(b,_):
        feats(pa_ref,b,vl,True)
        for c in range(16):
            h,m,l=split3(row8(vl,8*c))
            lf[b*16+c]=jnp.concatenate([h,h,m,m,h,l],0).astype(bf16)
        for c in range(0,16,2):
            d=pa_ref[b,8*c:8*c+16,:].astype(f32)
            da[b*16+c]=d[:8]; da[b*16+c+1]=d[8:]
        return 0
    lax.fori_loop(0,8,prep_a,0)
    def right(v):
        h,m,l=split3(v)
        return jnp.concatenate([h,m,h,m,l,h],0).T.astype(bf16)
    def prep_b(b,_):
        feats(pb_ref,b,vl,False)
        for c in range(16):
            rt[b*16+c]=right(row8(vl,8*c))
        for c in range(0,16,2):
            d=pb_ref[b,8*c:8*c+16,:].astype(f32)
            db[b*16+c]=d[:8]; db[b*16+c+1]=d[8:]
        return 0
    lax.fori_loop(0,2,prep_b,0)
    feats(own_ref,0,vl,False)
    for s in range(NSELF):
        c=4*y+s
        rt[32+s]=right(row8(vl,pl.multiple_of(8*c,8)))
        db[32+s]=da[own*16+c]
        ii[s]=own*16+c
        jj[s]=32+s
    rt[36]=rt[0]
    db[36]=jnp.zeros((8,256),f32)
    sa[...]=jnp.zeros_like(sa); sb[...]=jnp.zeros_like(sb)
    def comp(src,pos):
        base=(src//4)*16
        for zh in range(2):
            for k in range(4):
                ii[pos+k]=base+info[src,zh*4+k]
                jj[pos+k]=zh*16+info[src,8+zh*4+k]
            pos=pos+info[src,16+zh]
        return pos
    n=lax.fori_loop(0,32,comp,NSELF)
    for k in range(G):
        ii[n+k]=0; jj[n+k]=36
    steps=(n+G-1)//G
    def build(t,slot):
        for g in range(G):
            i=ii[t*G+g]; j=jj[t*G+g]
            d2=jnp.dot(rt[j],lf[i],preferred_element_type=f32)
            ub[slot,g]=lax.rsqrt(d2).astype(bf16)
    def apply(t,slot):
        for g in range(G):
            i=ii[t*G+g]; j=jj[t*G+g]
            u=ub[slot,g]
            r=jnp.dot(db[j].astype(bf16),u,preferred_element_type=f32)
            c=lax.dot_general(da[i].astype(bf16),u,(((1,),(1,)),((),())),preferred_element_type=f32)
            sa[i]=sa[i]+r
            sb[j]=sb[j]+c
    build(0,0)
    def step(t,_):
        slot=lax.rem(t,2)
        apply(t-1,1-slot)
        build(t,slot)
        return 0
    lax.fori_loop(1,steps,step,0)
    apply(steps-1,lax.rem(steps-1,2))
    def out_a(b,_):
        for c in range(0,16,2):
            acca_ref[b,8*c:8*c+16,:]=jnp.concatenate([sa[b*16+c],sa[b*16+c+1]],0).astype(bf16)
        return 0
    lax.fori_loop(0,8,out_a,0)
    accb_ref[...]=sb[0:32]

def near_call(info,pa,pb,own):
    V=pl.BlockSpec(memory_space=pltpu.VMEM)
    return pl.pallas_call(near_kernel,
        out_shape=(jax.ShapeDtypeStruct((8,128,256),bf16),jax.ShapeDtypeStruct((32,8,256),f32)),
        in_specs=[pl.BlockSpec(memory_space=pltpu.SMEM),V,V,V],out_specs=(V,V),
        scratch_shapes=[pltpu.VMEM((2,128,128),f32),pltpu.VMEM((NA,KF,256),bf16),pltpu.VMEM((NBT,256,KF),bf16),
            pltpu.VMEM((NA,8,256),f32),pltpu.VMEM((NBT,8,256),f32),pltpu.VMEM((NA,8,256),f32),pltpu.VMEM((NBT,8,256),f32),
            pltpu.VMEM((2,G,256,256),bf16),pltpu.SMEM((280,),jnp.int32),pltpu.SMEM((280,),jnp.int32)],
        compiler_params=pltpu.CompilerParams(vmem_limit_bytes=48*1024*1024),
    )(info,pa,pb,own)


MESH = pl.DeviceIdType.MESH
VM = pl.BlockSpec(memory_space=pltpu.VMEM)
SM = pl.BlockSpec(memory_space=pltpu.SMEM)


def coords():
    return tuple(lax.axis_index(n) for n in ("z", "x", "c", "y"))


def plane_peer(flat):
    return flat // 8, lax.rem(flat // 4, 2), lax.rem(flat, 4)


def gather_kernel(pack, info, pa, pb, got, ssem, rsem, isend, irecv, lsem):
    z, x, c, y = coords()
    me = (x * 2 + c) * 4 + y
    row = x * 2 + c
    barrier = pltpu.get_barrier_semaphore()

    def greet(t, _):
        px, pc, py = plane_peer(lax.rem(me + t, 32))
        pl.semaphore_signal(barrier, inc=1, device_id=(z, px, pc, py), device_id_type=MESH)
        return 0

    lax.fori_loop(1, 32, greet, 0)

    def greet_z(t, _):
        pl.semaphore_signal(barrier, inc=1, device_id=(lax.rem(z + t, 8), x, c, y), device_id_type=MESH)
        return 0

    lax.fori_loop(1, 8, greet_z, 0)
    own_a = pltpu.make_async_copy(pack, pa.at[row], lsem.at[0])
    own_a.start()
    own_i = pltpu.make_async_copy(info.at[me], got.at[me], lsem.at[1])
    own_i.start()
    owner = lax.rem(z, 4) == y
    half = z // 4

    @pl.when(owner)
    def _():
        cp = pltpu.make_async_copy(pack, pb.at[half], lsem.at[2])
        cp.start()
        cp.wait()

    pl.semaphore_wait(barrier, 38)

    def copy_b(t, h):
        return pltpu.make_async_remote_copy(
            src_ref=pack, dst_ref=pb.at[h], send_sem=ssem.at[8 + t], recv_sem=rsem.at[8 + h],
            device_id=(lax.rem(z + t, 8), x, c, y), device_id_type=MESH)

    @pl.when(owner)
    def _():
        def send(t, _):
            copy_b(t, half).start()
            return 0
        lax.fori_loop(1, 8, send, 0)

    def copy_a(t, slot):
        p = lax.rem(row + t, 8)
        return pltpu.make_async_remote_copy(
            src_ref=pack, dst_ref=pa.at[slot], send_sem=ssem.at[t], recv_sem=rsem.at[slot],
            device_id=(z, p // 2, lax.rem(p, 2), y), device_id_type=MESH)

    def send_a(t, _):
        copy_a(t, row).start()
        return 0

    lax.fori_loop(1, 8, send_a, 0)

    def copy_i(t, slot):
        p = lax.rem(me + t, 32)
        px, pc, py = plane_peer(p)
        return pltpu.make_async_remote_copy(
            src_ref=info.at[p], dst_ref=got.at[slot], send_sem=isend.at[t], recv_sem=irecv.at[slot],
            device_id=(z, px, pc, py), device_id_type=MESH)

    def send_i(t, _):
        copy_i(t, me).start()
        return 0

    lax.fori_loop(1, 32, send_i, 0)
    own_a.wait()
    own_i.wait()

    def wait_a(t, _):
        cp = copy_a(t, lax.rem(row + t, 8))
        cp.wait_send()
        cp.wait_recv()
        return 0

    lax.fori_loop(1, 8, wait_a, 0)

    def wait_i(t, _):
        cp = copy_i(t, lax.rem(me + t, 32))
        cp.wait_send()
        cp.wait_recv()
        return 0

    lax.fori_loop(1, 32, wait_i, 0)
    for h in range(2):
        @pl.when(jnp.logical_not(owner & (half == h)))
        def _(h=h):
            copy_b(1, h).wait_recv()

    @pl.when(owner)
    def _():
        def done(t, _):
            copy_b(t, half).wait_send()
            return 0
        lax.fori_loop(1, 8, done, 0)


def gather_call(pack, info):
    return pl.pallas_call(
        gather_kernel,
        out_shape=(jax.ShapeDtypeStruct((8, 192, 256), bf16), jax.ShapeDtypeStruct((2, 192, 256), bf16),
                   jax.ShapeDtypeStruct((32, 1, 128), jnp.int32)),
        in_specs=[VM, VM], out_specs=(VM, VM, VM),
        scratch_shapes=[pltpu.SemaphoreType.DMA((16,)), pltpu.SemaphoreType.DMA((10,)),
                        pltpu.SemaphoreType.DMA((32,)), pltpu.SemaphoreType.DMA((32,)),
                        pltpu.SemaphoreType.DMA((3,))],
        compiler_params=pltpu.CompilerParams(collective_id=1, has_side_effects=True),
    )(pack, info)


def reduce_kernel(acca, accb, far, out, ra, rb, total, ry, part, ssem, rsem, lsem):
    z, x, c, y = coords()
    row = x * 2 + c
    owner = lax.rem(z, 4) == y
    half = z // 4
    barrier = pltpu.get_barrier_semaphore()

    def peer_row(t):
        p = lax.rem(row + t, 8)
        return (z, p // 2, lax.rem(p, 2), y)

    def peer_y(t):
        return (z, x, c, lax.rem(y + t, 4))

    def greet(t, _):
        pl.semaphore_signal(barrier, inc=1, device_id=peer_row(t), device_id_type=MESH)
        return 0

    lax.fori_loop(1, 8, greet, 0)

    def greet_z(t, _):
        pl.semaphore_signal(barrier, inc=1, device_id=(lax.rem(z + t, 8), x, c, y), device_id_type=MESH)
        return 0

    lax.fori_loop(1, 8, greet_z, 0)

    def greet_y(t, _):
        pl.semaphore_signal(barrier, inc=1, device_id=peer_y(t), device_id_type=MESH)
        return 0

    lax.fori_loop(1, 4, greet_y, 0)
    pl.semaphore_wait(barrier, 17)

    def copy_a(t, slot):
        p = lax.rem(row + t, 8)
        return pltpu.make_async_remote_copy(
            src_ref=acca.at[p], dst_ref=ra.at[slot], send_sem=ssem.at[t], recv_sem=rsem.at[slot],
            device_id=peer_row(t), device_id_type=MESH)

    def copy_b(h, slot):
        return pltpu.make_async_remote_copy(
            src_ref=accb.at[h], dst_ref=rb.at[slot], send_sem=ssem.at[8 + h], recv_sem=rsem.at[8 + slot],
            device_id=(h * 4 + y, x, c, y), device_id_type=MESH)

    for h in range(2):
        @pl.when(jnp.logical_not(owner & (half == h)))
        def _(h=h):
            copy_b(h, z).start()

    def send_a(t, _):
        copy_a(t, row).start()
        return 0

    lax.fori_loop(1, 8, send_a, 0)
    total[...] = far[...] + acca[row].astype(f32)

    @pl.when(owner)
    def _():
        total[...] += accb[half].astype(f32)

    def recv_a(t, _):
        s = lax.rem(row + 8 - t, 8)
        copy_a(t, s).wait_recv()
        total[...] += ra[s].astype(f32)
        return 0

    lax.fori_loop(1, 8, recv_a, 0)

    @pl.when(owner)
    def _():
        def recv_b(t, _):
            s = lax.rem(z + t, 8)
            copy_b(0, s).wait_recv()
            total[...] += rb[s].astype(f32)
            return 0
        lax.fori_loop(1, 8, recv_b, 0)

    def copy_y(t, slot):
        q = lax.rem(y + t, 4)
        return pltpu.make_async_remote_copy(
            src_ref=total.at[pl.ds(pl.multiple_of(q * 32, 32), 32)], dst_ref=ry.at[slot],
            send_sem=ssem.at[10 + t], recv_sem=rsem.at[16 + slot],
            device_id=peer_y(t), device_id_type=MESH)

    for t in range(1, 4):
        copy_y(t, y).start()
    part[...] = total[pl.ds(pl.multiple_of(y * 32, 32), 32), :]
    for t in range(1, 4):
        s = lax.rem(y + t, 4)
        copy_y(t, s).wait_recv()
        part[...] += ry[s]

    def copy_o(t, slot):
        return pltpu.make_async_remote_copy(
            src_ref=part, dst_ref=out.at[pl.ds(pl.multiple_of(slot * 32, 32), 32)],
            send_sem=ssem.at[14 + t], recv_sem=rsem.at[20 + slot],
            device_id=peer_y(t), device_id_type=MESH)

    for t in range(1, 4):
        copy_o(t, y).start()
    own = pltpu.make_async_copy(part, out.at[pl.ds(pl.multiple_of(y * 32, 32), 32)], lsem)
    own.start()
    own.wait()

    for t in range(1, 4):
        copy_o(t, lax.rem(y + t, 4)).wait_recv()

    def done_a(t, _):
        copy_a(t, row).wait_send()
        return 0

    lax.fori_loop(1, 8, done_a, 0)
    for h in range(2):
        @pl.when(jnp.logical_not(owner & (half == h)))
        def _(h=h):
            copy_b(h, z).wait_send()
    for t in range(1, 4):
        copy_y(t, y).wait_send()
        copy_o(t, y).wait_send()


def reduce_call(acca, accb, far):
    return pl.pallas_call(
        reduce_kernel,
        out_shape=jax.ShapeDtypeStruct((128, 256), f32),
        in_specs=[VM, VM, VM], out_specs=VM,
        scratch_shapes=[pltpu.VMEM((8, 128, 256), bf16), pltpu.VMEM((8, 128, 256), bf16),
                        pltpu.VMEM((128, 256), f32), pltpu.VMEM((4, 32, 256), f32), pltpu.VMEM((32, 256), f32),
                        pltpu.SemaphoreType.DMA((18,)), pltpu.SemaphoreType.DMA((24,)), pltpu.SemaphoreType.DMA],
        compiler_params=pltpu.CompilerParams(collective_id=2, has_side_effects=True),
    )(acca, accb, far)


def block_mask(parts):
    r = lax.broadcasted_iota(jnp.int32, (64, 256), 0) // 8
    k = lax.broadcasted_iota(jnp.int32, (64, 256), 1) // 32
    return jnp.where(r == k, 1.0, 0.0)


def through(dens, first, second, mask):
    p = lax.dot_general(dens, first, (((1,), (1,)), ((), ())), preferred_element_type=f32)
    p = (p.astype(bf16).astype(f32) * mask).astype(bf16)
    return jnp.dot(p, second, preferred_element_type=f32)


def place(e):
    z = e // 8
    return (lax.rem(e, 8) * 4 + lax.rem(z, 4)) * 2 + z // 4


def far_cols_kernel(pairs, counts, left, right, dens, out, d32):
    for k in range(8):
        v = dens[16 * k:16 * k + 16, :].astype(f32)
        d32[2 * k] = v[:8]
        d32[2 * k + 1] = v[8:]
    mask = block_mask(8)

    def step(b, _):
        rows = pl.ds(pl.multiple_of(b * 256, 256), 256)
        ds = []
        for s in range(8):
            e, k = b * 4 + s // 2, s % 2
            i = lax.rem(pairs[e, 2 * k], 16)
            ds.append(jnp.where(k < counts[e], d32[i], 0.0))
        r = through(jnp.concatenate(ds, 0).astype(bf16), left[rows, :], right[rows, :], mask)
        for s in range(4):
            o = place(b * 4 + s) * 16
            out[pl.ds(pl.multiple_of(o, 16), 16), :] = r[16 * s:16 * s + 16].astype(bf16)
        return 0

    lax.fori_loop(0, 16, step, 0, unroll=2)


def far_cols_call(pairs, counts, left, right, dens):
    return pl.pallas_call(
        far_cols_kernel,
        out_shape=jax.ShapeDtypeStruct((1024, 256), bf16),
        in_specs=[SM, SM, VM, VM, VM], out_specs=VM,
        scratch_shapes=[pltpu.VMEM((16, 8, 256), f32)],
        compiler_params=pltpu.CompilerParams(vmem_limit_bytes=32 * 1024 * 1024),
    )(pairs, counts, left, right, dens)


def pick_kernel(info, pb, out, d32):
    for h in range(2):
        for k in range(8):
            v = pb[h, 16 * k:16 * k + 16, :].astype(f32)
            d32[16 * h + 2 * k] = v[:8]
            d32[16 * h + 2 * k + 1] = v[8:]

    def step(s, _):
        for h in range(2):
            a = info[s, 18 + 2 * h]
            b = info[s, 19 + 2 * h]
            v = jnp.concatenate([d32[h * 16 + a], d32[h * 16 + b]], 0).astype(bf16)
            out[pl.ds(pl.multiple_of(s * 32 + 16 * h, 16), 16), :] = v
        return 0

    lax.fori_loop(0, 32, step, 0, unroll=4)


def pick_call(info, pb):
    return pl.pallas_call(
        pick_kernel,
        out_shape=jax.ShapeDtypeStruct((1024, 256), bf16),
        in_specs=[SM, VM], out_specs=VM,
        scratch_shapes=[pltpu.VMEM((32, 8, 256), f32)],
        compiler_params=pltpu.CompilerParams(vmem_limit_bytes=32 * 1024 * 1024),
    )(info, pb)


def far_rows_kernel(pairs, counts, info, left, right, dens, cols, accb_in, rows_out, cols_out, acc, accb):
    mask = block_mask(8)
    acc[...] = jnp.zeros_like(acc)
    accb[...] = accb_in[...]

    def step(b, _):
        rows = pl.ds(pl.multiple_of(b * 256, 256), 256)
        ds = []
        for s in range(4):
            o = place(b * 4 + s) * 16
            ds.append(dens[pl.ds(pl.multiple_of(o, 16), 16), :])
        r = through(jnp.concatenate(ds, 0), right[rows, :], left[rows, :], mask)
        for s in range(8):
            e, k = b * 4 + s // 2, s % 2
            i = lax.rem(pairs[e, 2 * k], 16)
            acc[i] += jnp.where(k < counts[e], r[8 * s:8 * s + 8], 0.0)
        return 0

    lax.fori_loop(0, 16, step, 0, unroll=2)

    def add(s, _):
        for h in range(2):
            v = cols[pl.ds(pl.multiple_of(s * 32 + 16 * h, 16), 16), :].astype(f32)
            accb[h * 16 + info[s, 18 + 2 * h]] += v[:8]
            accb[h * 16 + info[s, 19 + 2 * h]] += v[8:]
        return 0

    lax.fori_loop(0, 32, add, 0, unroll=4)
    for k in range(16):
        rows_out[8 * k:8 * k + 8, :] = acc[k]
    for h in range(2):
        for k in range(8):
            cols_out[h, 16 * k:16 * k + 16, :] = jnp.concatenate(
                [accb[16 * h + 2 * k], accb[16 * h + 2 * k + 1]], 0).astype(bf16)


def far_rows_call(pairs, counts, info, left, right, dens, cols, accb):
    return pl.pallas_call(
        far_rows_kernel,
        out_shape=(jax.ShapeDtypeStruct((128, 256), f32), jax.ShapeDtypeStruct((2, 128, 256), bf16)),
        in_specs=[SM, SM, SM, VM, VM, VM, VM, VM], out_specs=(VM, VM),
        scratch_shapes=[pltpu.VMEM((16, 8, 256), f32), pltpu.VMEM((32, 8, 256), f32)],
        compiler_params=pltpu.CompilerParams(vmem_limit_bytes=32 * 1024 * 1024),
    )(pairs, counts, info, left, right, dens, cols, accb)


def per_device(density, positions, areas, near_pairs, near_counts, far_pairs, far_counts, far_right, far_left):
    pack = jnp.concatenate(
        [density.reshape(128, 256), positions.transpose(1, 0, 2).reshape(48, 256), areas], axis=0)
    near = near_pairs.reshape(2, 4, 4, 2, 4, 2)
    near = near.transpose(2, 3, 1, 5, 0, 4).reshape(32, 16) % 16
    ncnt = near_counts.reshape(2, 4, 4, 2).transpose(2, 3, 1, 0).reshape(32, 2)
    fcol = far_pairs[..., 1].reshape(2, 4, 4, 2, 2).transpose(2, 3, 1, 0, 4).reshape(32, 4) % 16
    info = jnp.concatenate([near, ncnt, fcol, jnp.zeros((32, 106), jnp.int32)], axis=1).reshape(32, 1, 128)
    pairs = far_pairs.reshape(64, 4)
    counts = far_counts.reshape(64)
    left = far_left.reshape(4096, 256)
    right = far_right.reshape(4096, 256)

    cols = far_cols_call(pairs, counts, left, right, pack[:128])
    cols = lax.all_to_all(cols.reshape(32, 32, 256), ("x", "c", "y"), 0, 0, tiled=True).reshape(1024, 256)
    pa, pb, got = gather_call(pack, info)
    got = got.reshape(32, 128)
    dens = pick_call(got, pb)
    dens = lax.all_to_all(dens.reshape(32, 32, 256), ("x", "c", "y"), 0, 0, tiled=True).reshape(1024, 256)
    acca, accb = near_call(got, pa, pb, pack[None])
    rows, accb = far_rows_call(pairs, counts, got, left, right, dens, cols, accb)
    out = reduce_call(acca, accb, rows)
    return out.reshape(16, 8, 256)


def solution(mesh):
    grid = Mesh(mesh.devices.reshape(8, 4, 2, 4), ("z", "x", "c", "y"))
    d = ("z", "x", "c")
    return jax.shard_map(
        per_device,
        mesh=grid,
        in_specs=(
            P(d, None, None),
            P(d, None, None),
            P(d, None),
            P(d, "y", None, None, None),
            P(d, "y", None),
            P(d, "y", None, None, None),
            P(d, "y", None),
            P(d, "y", None, None, None, None),
            P(d, "y", None, None, None, None),
        ),
        out_specs=P(d, None, None),
        check_vma=False,
    )
```

```python
import jax
import jax.numpy as jnp
from jax import lax
from jax.experimental import pallas as pl
from jax.experimental.pallas import tpu as pltpu
from jax.sharding import Mesh, PartitionSpec as P

f32 = jnp.float32
bf16 = jnp.bfloat16
i32 = jnp.int32
MESH = pl.DeviceIdType.MESH
KF = 48


def rem(a, n):
    return lax.rem(a, jnp.int32(n))


def plane_peer(flat):
    return flat // 8, rem(flat // 4, 2), rem(flat, 4)


def split3(v):
    h = v.astype(bf16).astype(f32)
    m = (v - h).astype(bf16).astype(f32)
    return h, m, v - h - m


def feats(load, vref, left):
    xs = [load(128 + 16 * k).astype(f32) - 0.5 for k in range(3)]
    a = load(176).astype(f32)
    w = 256.0 / (a * a)
    n = (xs[0] * xs[0] + xs[1] * xs[1] + xs[2] * xs[2] + 0.005) * w
    rows = [n, w] if left else [w, n]
    rows += [v * ((-2.0 if left else 1.0) * w) for v in xs]
    for k, r in enumerate(rows):
        vref[0, pl.ds(k, 16, stride=8), :] = r[:, :128]
        vref[1, pl.ds(k, 16, stride=8), :] = r[:, 128:]


def rows8(vref, c):
    o = pl.ds(pl.multiple_of(8 * c, 8), 8)
    return jnp.concatenate([vref[0, o, :], vref[1, o, :]], 1)


def left_factor(v):
    h, m, l = split3(v)
    return jnp.concatenate([h, h, m, m, h, l], 0).astype(bf16)


def right_factor(v):
    h, m, l = split3(v)
    return jnp.concatenate([h, m, h, m, l, h], 0).T.astype(bf16)


def through(dens, first, second, mask):
    p = lax.dot_general(dens, first, (((1,), (1,)), ((), ())), preferred_element_type=f32)
    p = (p.astype(bf16).astype(f32) * mask).astype(bf16)
    return jnp.dot(p, second, preferred_element_type=f32)


def pick_matrix(ids, rows):
    lane = lax.broadcasted_iota(i32, (1, 256), 1)
    key = jnp.full((1, 256), -8, i32)
    for n, v in enumerate(ids):
        key = jnp.where(lane // 8 == n, v * 8, key)
    key = key + rem(lane, 8)
    return jnp.where(lax.broadcasted_iota(i32, (rows, 256), 0) == key, 1.0, 0.0).astype(bf16)


def gathered(sel, v):
    hi = v.astype(bf16)
    lo = (v - hi.astype(f32)).astype(bf16)
    return jnp.dot(sel, hi, preferred_element_type=f32) + jnp.dot(sel, lo, preferred_element_type=f32)


def kernel(near, ncnt, far, dens, pos, area, fars, fcnts, left_h, right_h, out,
           left, right, pack, pa, pb, t1, t2, isrc, igot, cvm, csm, vl, lf, rt, da, db, dself, ub, rbuf, cbuf,
           acc_b, own, fc, fcr, fd, fdr, sa, sb, ra, rb, part,
           lsem, s_a, r_a, s_b, r_b, s_i, r_i, s_fc, r_fc, s_fd, r_fd, s_oa, r_oa, s_ob, r_ob, s_o, r_o):
    z, x, c, y = (lax.axis_index(n) for n in ("z", "x", "c", "y"))
    row = x * 2 + c
    me = row * 4 + y
    owner = rem(z, 4) == y
    half = z // 4
    zy = rem(z, 4)

    def each(lo, hi, f):
        def body(t, _):
            f(t)
            return 0
        lax.fori_loop(lo, hi, body, 0)

    cl = pltpu.make_async_copy(left_h, left, lsem.at[0])
    cr = pltpu.make_async_copy(right_h, right, lsem.at[1])
    cl.start()
    cr.start()

    barrier = pltpu.get_barrier_semaphore()

    def greet(dev):
        pl.semaphore_signal(barrier, inc=1, device_id=dev, device_id_type=MESH)

    def plane_dev(q):
        px, pc, py = plane_peer(q)
        return (z, px, pc, py)

    each(1, 32, lambda t: greet(plane_dev(rem(me + t, 32))))
    each(1, 8, lambda t: greet((rem(z + t, 8), x, c, zy)))
    for h in range(2):
        @pl.when(z != h * 4 + y)
        def _(h=h):
            greet((h * 4 + y, x, c, y))

    pack[0:128, :] = dens[...]
    pack[128:176, :] = pos[...]
    pack[176:192, :] = area[...]
    t1[...] = jnp.zeros_like(t1)
    t2[...] = jnp.zeros_like(t2)
    t1[:, 0:64] = near[...]
    t2[0:1, 0:64] = ncnt[...]
    t2[1:2, 0:64] = far[1:2, :]
    t2[2:3, 0:64] = far[3:4, :]
    lane8 = lax.broadcasted_iota(i32, (8, 128), 1)
    isrc[...] = jnp.where(lane8 < 64, t1[...], pltpu.roll(t2[...], 64, 1))
    igot[me] = isrc[...]

    @pl.when(owner)
    def _():
        pb[half] = pack[...]
        pl.semaphore_wait(barrier, 42)

    @pl.when(jnp.logical_not(owner))
    def _():
        pl.semaphore_wait(barrier, 39)

    def remote(src, dst, ss, rs, dev):
        return pltpu.make_async_remote_copy(src_ref=src, dst_ref=dst, send_sem=ss, recv_sem=rs,
                                            device_id=dev, device_id_type=MESH)

    def copy_b(t, h):
        return remote(pack, pb.at[h], s_b.at[t], r_b.at[h], (rem(z + t, 8), x, c, y))

    @pl.when(owner)
    def _():
        each(1, 8, lambda t: copy_b(t, half).start())

    def copy_i(t, slot):
        return remote(isrc, igot.at[slot], s_i.at[t], r_i.at[slot], plane_dev(rem(me + t, 32)))

    each(1, 32, lambda t: copy_i(t, me).start())

    def copy_a(t, slot):
        p = rem(row + 8 - t, 8)
        return remote(pack, pa.at[slot], s_a.at[t], r_a.at[slot], (z, p // 2, rem(p, 2), y))

    each(1, 8, lambda t: copy_a(t, row).start())

    def tables(load, dref, base):
        for k in range(8):
            v = load(16 * k).astype(f32)
            dref[base + 2 * k] = v[:8]
            dref[base + 2 * k + 1] = v[8:]

    vl[...] = jnp.zeros_like(vl)
    tables(lambda o: pack[o:o + 16, :], da, 0)
    kr = lax.broadcasted_iota(i32, (64, 256), 0) // 8
    kc = lax.broadcasted_iota(i32, (64, 256), 1) // 32
    mask = jnp.where(kr == kc, 1.0, 0.0)

    def far_owner(q, h):
        return h * 32 + rem(q, 4) * 8 + q // 4

    def copy_fc(q, slot):
        return remote(fc.at[q], fcr.at[slot], s_fc.at[q], r_fc.at[slot], plane_dev(q))

    cl.wait()
    cr.wait()

    def far_cols(t):
        qs = [rem(me + 2 * t, 32), rem(me + 2 * t + 1, 32)]
        es = [far_owner(q, h) for q in qs for h in range(2)]
        ds = []
        for e in es:
            for k in range(2):
                i = rem(fars[2 * k, e], 16)
                ds.append(jnp.where(k < fcnts[0, e], da[i], 0.0))
        r = through(jnp.concatenate(ds, 0).astype(bf16), jnp.concatenate([left[e] for e in es], 0),
                    jnp.concatenate([right[e] for e in es], 0), mask).astype(bf16)
        fc[qs[0]] = r[:32]
        fc[qs[1]] = r[32:]

        @pl.when(t > 0)
        def _():
            copy_fc(qs[0], me).start()

        copy_fc(qs[1], me).start()

    each(0, 16, far_cols)
    fcr[me] = fc[me]

    def prep(load, par):
        feats(load, vl, True)
        for k in range(16):
            lf[par * 16 + k] = left_factor(rows8(vl, k))
        tables(load, da, par * 16)

    prep(lambda o: pack[o:o + 16, :], 0)
    feats(lambda o: pack[o:o + 16, :], vl, False)
    own[...] = jnp.zeros_like(own)
    for s in range(4):
        k = 4 * y + s
        u = lax.rsqrt(jnp.dot(right_factor(rows8(vl, k)), lf[k], preferred_element_type=f32)).astype(bf16)
        own[pl.ds(pl.multiple_of(8 * k, 8), 8), :] = jnp.dot(da[k].astype(bf16), u, preferred_element_type=f32)

    each(1, 32, lambda t: copy_i(t, rem(me + t, 32)).wait_recv())
    q0 = y * 8 + row
    lists = jnp.zeros((8, 128), i32)
    for s in range(32):
        lists = jnp.where(rem(lane8, 32) == s, pltpu.roll(igot[s], rem(s - q0 + 128, 128), 1), lists)
    cvm[...] = lists
    ci = pltpu.make_async_copy(cvm, csm, lsem.at[0])
    ci.start()
    for h in range(2):
        @pl.when(z != h * 4 + y)
        def _(h=h):
            copy_b(1, h).wait_recv()
    for h in range(2):
        feats(lambda o, h=h: pb[h, o:o + 16, :], vl, False)
        for k in range(16):
            rt[h * 16 + k] = right_factor(rows8(vl, k))
        tables(lambda o, h=h: pb[h, o:o + 16, :], db, h * 16)
    ci.wait()

    def far_col(s, h, k):
        return h * 16 + rem(csm[1 + k, 64 + h * 32 + s], 16)

    def copy_fd(s, slot):
        return remote(fd.at[s], fdr.at[slot], s_fd.at[s], r_fd.at[slot], plane_dev(s))

    def send_fd(t):
        s = rem(me + t, 32)
        fd[s] = jnp.concatenate([db[far_col(s, h, k)] for h in range(2) for k in range(2)], 0).astype(bf16)

        @pl.when(t > 0)
        def _():
            copy_fd(s, me).start()

    each(0, 32, send_fd)
    fdr[me] = fd[me]

    def slot_ids(b, n):
        s, h, k = 4 * b + n // 8, (n // 4) % 2, n % 4
        return (rem(csm[2 * k, h * 32 + s], 16), h * 16 + rem(csm[2 * k + 1, h * 32 + s], 16),
                k < csm[0, 64 + h * 32 + s])

    def build(b, par, first, slot):
        for g in range(16):
            i, j, _ = slot_ids(b, first + g)
            d2 = jnp.dot(rt[j], lf[par * 16 + i], preferred_element_type=f32)
            ub[slot, g] = lax.rsqrt(d2).astype(bf16)

    def apply(b, par, first, slot):
        for g in range(16):
            n = first + g
            i, j, _ = slot_ids(b, n)
            u = ub[slot, g]
            rbuf[8 * n:8 * n + 8, :] = jnp.dot(db[j].astype(bf16), u, preferred_element_type=f32)
            cbuf[8 * n:8 * n + 8, :] = lax.dot_general(
                da[par * 16 + i].astype(bf16), u, (((1,), (1,)), ((), ())), preferred_element_type=f32)

    def copy_oa(b, yy, slot):
        return remote(sa.at[b, pl.ds(pl.multiple_of(yy * 32, 32), 32)], ra.at[slot], s_oa.at[b * 4 + yy], r_oa.at[slot],
                      (z, b // 2, rem(b, 2), yy))

    def sums(b):
        ids = [slot_ids(b, n) for n in range(32)]
        a = gathered(pick_matrix([jnp.where(v[2], v[0], -1) for v in ids], 128), rbuf[...])
        acc_b[...] += gathered(pick_matrix([jnp.where(v[2], v[1], -1) for v in ids], 256), cbuf[...])
        return a

    def finish(b):
        sa[b] = sums(b).astype(bf16)
        each(0, 4, lambda v: copy_oa(b, rem(y + v, 4), me).start())

    acc_b[...] = jnp.zeros_like(acc_b)
    build(row, 0, 0, 0)

    def group(t):
        b = rem(row + t, 8)
        nb = rem(row + t + 1, 8)
        par = rem(t, 2)
        copy_a(t + 1, nb).wait_recv()
        apply(b, par, 0, 0)
        build(b, par, 16, 1)
        prep(lambda o: pa[nb, o:o + 16, :], 1 - par)
        apply(b, par, 16, 1)
        build(nb, 1 - par, 0, 0)

        @pl.when(t == 0)
        def _():
            own[...] += sums(b)

        @pl.when(t > 0)
        def _():
            finish(b)

    each(0, 7, group)
    last = rem(row + 7, 8)
    apply(last, 1, 0, 0)
    build(last, 1, 16, 1)
    apply(last, 1, 16, 1)
    finish(last)

    def wait_fc(t):
        q = rem(me + t, 32)
        copy_fc(q, q).wait_recv()

    each(1, 32, wait_fc)

    def add_cols(g):
        ids = [far_col(g * 8 + n // 4, (n // 2) % 2, n % 2) for n in range(32)]
        v = jnp.concatenate([fcr[g * 8 + k] for k in range(8)], 0)
        acc_b[...] += jnp.dot(pick_matrix(ids, 256), v, preferred_element_type=f32)

    each(0, 4, add_cols)
    for h in range(2):
        sb[h] = acc_b[128 * h:128 * h + 128, :].astype(bf16)

    def copy_ob(h, yy, slot):
        return remote(sb.at[h, pl.ds(pl.multiple_of(yy * 32, 32), 32)], rb.at[slot], s_ob.at[h * 4 + yy], r_ob.at[slot],
                      (h * 4 + y, x, c, yy))

    def all_ob(f):
        for h in range(2):
            for v in range(4):
                yy = rem(y + v, 4)
                if v == 0:
                    @pl.when(z != h * 4 + y)
                    def _(h=h, yy=yy):
                        f(copy_ob(h, yy, z))
                else:
                    f(copy_ob(h, yy, z))

    all_ob(lambda cp: cp.start())

    @pl.when(owner)
    def _():
        rb[z] = sb[half, pl.ds(pl.multiple_of(y * 32, 32), 32), :]

    def wait_fd(t):
        q = rem(me + t, 32)
        copy_fd(q, q).wait_recv()

    each(1, 32, wait_fd)

    def far_rows(g):
        ids = []
        for b in range(4):
            qs = [g * 8 + 2 * b, g * 8 + 2 * b + 1]
            es = [far_owner(q, h) for q in qs for h in range(2)]
            rbuf[64 * b:64 * b + 64, :] = through(
                jnp.concatenate([fdr[q] for q in qs], 0), jnp.concatenate([right[e] for e in es], 0),
                jnp.concatenate([left[e] for e in es], 0), mask)
            ids += [jnp.where(k < fcnts[0, e], rem(fars[2 * k, e], 16), -1) for e in es for k in range(2)]
        own[...] += gathered(pick_matrix(ids, 128), rbuf[...])

    each(0, 4, far_rows)

    sa[row] = own[...].astype(bf16)
    each(1, 4, lambda v: copy_oa(row, rem(y + v, 4), me).start())
    part[...] = own[pl.ds(pl.multiple_of(y * 32, 32), 32), :]

    def add_a(t):
        q = rem(me + t, 32)
        copy_oa(row, y, q).wait_recv()
        part[...] += ra[q].astype(f32)

    each(1, 32, add_a)

    def add_b(t):
        s = rem(z + t, 8)

        @pl.when(jnp.logical_not(owner & (s == z)))
        def _():
            copy_ob(half, y, s).wait_recv()

        part[...] += rb[s].astype(f32)

    each(0, 8, add_b)

    def copy_o(t, slot):
        return remote(part, out.at[pl.ds(pl.multiple_of(slot * 32, 32), 32)], s_o.at[t], r_o.at[slot],
                      (z, x, c, rem(y + t, 4)))

    each(1, 4, lambda t: copy_o(t, y).start())
    out[pl.ds(pl.multiple_of(y * 32, 32), 32), :] = part[...]

    def sent_plane(t):
        q = rem(me + t, 32)
        copy_i(t, me).wait_send()
        copy_fc(q, me).wait_send()
        copy_fd(q, me).wait_send()

    each(1, 32, sent_plane)
    each(1, 8, lambda t: copy_a(t, row).wait_send())

    @pl.when(owner)
    def _():
        each(1, 8, lambda t: copy_b(t, half).wait_send())

    def sent_oa(t):
        b = rem(row + t, 8)
        each(0, 4, lambda v: copy_oa(b, rem(y + v, 4), me).wait_send())

    each(1, 8, sent_oa)
    each(1, 4, lambda v: copy_oa(row, rem(y + v, 4), me).wait_send())
    all_ob(lambda cp: cp.wait_send())
    each(1, 4, lambda t: copy_o(t, rem(y + t, 4)).wait_recv())
    each(1, 4, lambda t: copy_o(t, y).wait_send())


def per_device(density, positions, areas, near_pairs, near_counts, far_pairs, far_counts, far_right, far_left):
    near = near_pairs[0, 0].transpose(1, 2, 0).reshape(8, 64)
    far = far_pairs[0, 0].transpose(1, 2, 0).reshape(4, 64)
    ncnt = near_counts.reshape(1, 64)
    fcnt = far_counts.reshape(1, 64)
    left = far_left.reshape(64, 64, 256)
    right = far_right.reshape(64, 64, 256)
    vm = pl.BlockSpec(memory_space=pltpu.VMEM)
    sm = pl.BlockSpec(memory_space=pltpu.SMEM)
    hbm = pl.BlockSpec(memory_space=pl.ANY)
    V, D = pltpu.VMEM, pltpu.SemaphoreType.DMA
    out = pl.pallas_call(
        kernel,
        out_shape=jax.ShapeDtypeStruct((128, 256), f32),
        in_specs=[vm] * 6 + [sm] * 2 + [hbm] * 2,
        out_specs=vm,
        scratch_shapes=[
            V((64, 64, 256), bf16), V((64, 64, 256), bf16), V((192, 256), bf16), V((8, 192, 256), bf16),
            V((2, 192, 256), bf16), V((8, 128), i32), V((8, 128), i32), V((8, 128), i32), V((32, 8, 128), i32),
            V((8, 128), i32), pltpu.SMEM((8, 128), i32), V((2, 128, 128), f32), V((32, KF, 256), bf16),
            V((32, 256, KF), bf16), V((32, 8, 256), f32), V((32, 8, 256), f32), V((16, 8, 256), f32),
            V((2, 16, 256, 256), bf16), V((256, 256), f32), V((256, 256), f32),
            V((256, 256), f32), V((128, 256), f32), V((32, 32, 256), bf16), V((32, 32, 256), bf16),
            V((32, 32, 256), bf16), V((32, 32, 256), bf16), V((8, 128, 256), bf16), V((2, 128, 256), bf16),
            V((32, 32, 256), bf16), V((8, 32, 256), bf16), V((32, 256), f32),
            D((2,)), D((8,)), D((8,)), D((8,)), D((2,)), D((32,)), D((32,)), D((32,)), D((32,)), D((32,)), D((32,)),
            D((32,)), D((32,)), D((8,)), D((8,)), D((4,)), D((4,)),
        ],
        compiler_params=pltpu.CompilerParams(collective_id=1, has_side_effects=True,
                                             vmem_limit_bytes=56 * 1024 * 1024),
    )(near, ncnt, far, density.reshape(128, 256), positions.transpose(1, 0, 2).reshape(48, 256), areas,
      far, fcnt, left, right)
    return out.reshape(16, 8, 256)


def solution(mesh):
    grid = Mesh(mesh.devices.reshape(8, 4, 2, 4), ("z", "x", "c", "y"))
    d = ("z", "x", "c")
    return jax.shard_map(
        per_device,
        mesh=grid,
        in_specs=(
            P(d, None, None),
            P(d, None, None),
            P(d, None),
            P(d, "y", None, None, None),
            P(d, "y", None),
            P(d, "y", None, None, None),
            P(d, "y", None),
            P(d, "y", None, None, None, None),
            P(d, "y", None, None, None, None),
        ),
        out_specs=P(d, None, None),
        check_vma=False,
    )
```

```python
import jax
import jax.numpy as jnp
from jax import lax
from jax.experimental import pallas as pl
from jax.experimental.pallas import tpu as pltpu
from jax.sharding import Mesh, PartitionSpec as P

f32 = jnp.float32
bf16 = jnp.bfloat16
i32 = jnp.int32
MESH = pl.DeviceIdType.MESH
KF = 48


def rem(a, n):
    return lax.rem(a, jnp.int32(n))


def plane_peer(flat):
    return flat // 8, rem(flat // 4, 2), rem(flat, 4)


def split3(v):
    h = v.astype(bf16).astype(f32)
    m = (v - h).astype(bf16).astype(f32)
    return h, m, v - h - m


def feats(load, vref, left):
    xs = [load(128 + 16 * k).astype(f32) - 0.5 for k in range(3)]
    a = load(176).astype(f32)
    w = 256.0 / (a * a)
    n = (xs[0] * xs[0] + xs[1] * xs[1] + xs[2] * xs[2] + 0.005) * w
    rows = [n, w] if left else [w, n]
    rows += [v * ((-2.0 if left else 1.0) * w) for v in xs]
    for k, r in enumerate(rows):
        vref[0, pl.ds(k, 16, stride=8), :] = r[:, :128]
        vref[1, pl.ds(k, 16, stride=8), :] = r[:, 128:]


def rows8(vref, c):
    o = pl.ds(pl.multiple_of(8 * c, 8), 8)
    return jnp.concatenate([vref[0, o, :], vref[1, o, :]], 1)


def left_factor(v):
    h, m, l = split3(v)
    return jnp.concatenate([h, h, m, m, h, l], 0).astype(bf16)


def right_factor(v):
    h, m, l = split3(v)
    return jnp.concatenate([h, m, h, m, l, h], 0).T.astype(bf16)


def through(dens, first, second, mask):
    p = lax.dot_general(dens, first, (((1,), (1,)), ((), ())), preferred_element_type=f32)
    p = (p.astype(bf16).astype(f32) * mask).astype(bf16)
    return jnp.dot(p, second, preferred_element_type=f32)


def pick_matrix(ids, rows):
    lane = lax.broadcasted_iota(i32, (1, 256), 1)
    key = jnp.full((1, 256), -8, i32)
    for n, v in enumerate(ids):
        key = jnp.where(lane // 8 == n, v * 8, key)
    key = key + rem(lane, 8)
    return jnp.where(lax.broadcasted_iota(i32, (rows, 256), 0) == key, 1.0, 0.0).astype(bf16)


def gathered(sel, v):
    hi = v.astype(bf16)
    lo = (v - hi.astype(f32)).astype(bf16)
    return jnp.dot(sel, hi, preferred_element_type=f32) + jnp.dot(sel, lo, preferred_element_type=f32)


def kernel(near, ncnt, far, dens, pos, area, fars, fcnts, left_h, right_h, out,
           left, right, pack, pa, pb, t1, t2, igy, igot, cvm, csm, vl, lf, rt, da, db, ub, rbuf, cbuf,
           acc_b, own, fc, fcy, fcr, fd, fdy, fdr, sa, sb, ra, rb, part,
           lsem, s_a, r_a, s_b, r_b, s_y, r_y, s_r, r_r, s_oa, r_oa, s_ob, r_ob, s_o, r_o):
    z, x, c, y = (lax.axis_index(n) for n in ("z", "x", "c", "y"))
    row = x * 2 + c
    me = row * 4 + y
    half = z // 4
    zy = rem(z, 4)
    owner = zy == y

    def each(lo, hi, f):
        def body(t, _):
            f(t)
            return 0
        lax.fori_loop(lo, hi, body, 0)

    cl = pltpu.make_async_copy(left_h, left, lsem.at[0])
    cr = pltpu.make_async_copy(right_h, right, lsem.at[1])
    cl.start()
    cr.start()

    barrier = pltpu.get_barrier_semaphore()

    def greet(dev):
        pl.semaphore_signal(barrier, inc=1, device_id=dev, device_id_type=MESH)

    def plane_dev(q):
        px, pc, py = plane_peer(q)
        return (z, px, pc, py)

    each(1, 32, lambda t: greet(plane_dev(rem(me + t, 32))))
    each(1, 8, lambda t: greet((rem(z + t, 8), x, c, zy)))
    for h in range(2):
        @pl.when(z != h * 4 + y)
        def _(h=h):
            for v in range(4):
                greet((h * 4 + y, x, c, v))

    pack[0:128, :] = dens[...]
    pack[128:176, :] = pos[...]
    pack[176:192, :] = area[...]
    t1[...] = jnp.zeros_like(t1)
    t2[...] = jnp.zeros_like(t2)
    t1[:, 0:64] = near[...]
    t2[0:1, 0:64] = ncnt[...]
    t2[1:2, 0:64] = far[1:2, :]
    t2[2:3, 0:64] = far[3:4, :]
    lane8 = lax.broadcasted_iota(i32, (8, 128), 1)
    igy[y] = jnp.where(lane8 < 64, t1[...], pltpu.roll(t2[...], 64, 1))

    def quarter(n):
        return pl.ds(pl.multiple_of(y * n, n), n)

    @pl.when(owner)
    def _():
        pb[half, quarter(48), :] = pack[quarter(48), :]
        pl.semaphore_wait(barrier, 42)

    @pl.when(jnp.logical_not(owner))
    def _():
        pl.semaphore_wait(barrier, 46)

    def remote(src, dst, ss, rs, dev):
        return pltpu.make_async_remote_copy(src_ref=src, dst_ref=dst, send_sem=ss, recv_sem=rs,
                                            device_id=dev, device_id_type=MESH)

    side = (z, x, c, rem(y + 1, 4))

    def copy_b(t):
        return remote(pack.at[quarter(48)], pb.at[half, quarter(48)], s_b, r_b.at[half], (rem(z + t, 8), x, c, zy))

    for t in (4, 3, 5, 2, 6, 1, 7):
        copy_b(t).start()

    @pl.when(jnp.logical_not(owner))
    def _():
        copy_b(0).start()

    def step_y(src, dst, k):
        for t in range(1, 4):
            yy = rem(y + t, 4)
            remote(src(yy), dst.at[y], s_y.at[k], r_y.at[k], (z, x, c, yy)).start()

    def wait_y(dst, k):
        w = dst.at[pl.ds(0, 3)]
        remote(w, w, s_y.at[k], r_y.at[k], side).wait_recv()

    def step_row(src, dst, k):
        def one(t):
            p = rem(row + 8 - t, 8)
            remote(src.at[:, p], dst.at[row], s_r.at[k], r_r.at[k], (z, p // 2, rem(p, 2), y)).start()
        each(1, 8, one)

    def wait_row(dst, k):
        w = dst.at[pl.ds(0, 7)]
        remote(w, w, s_r.at[k], r_r.at[k], side).wait_recv()

    step_y(lambda yy: igy.at[y], igy, 0)

    def copy_a(t, slot):
        p = rem(row + 8 - t, 8)
        return remote(pack, pa.at[slot], s_a, r_a.at[slot], (z, p // 2, rem(p, 2), y))

    def tables(load, dref, base):
        for k in range(8):
            v = load(16 * k).astype(f32)
            dref[base + 2 * k] = v[:8]
            dref[base + 2 * k + 1] = v[8:]

    def prep(load, par):
        feats(load, vl, True)
        for k in range(16):
            lf[par * 16 + k] = left_factor(rows8(vl, k))
        tables(load, da, par * 16)

    vl[...] = jnp.zeros_like(vl)
    prep(lambda o: pack[o:o + 16, :], 0)
    feats(lambda o: pack[o:o + 16, :], vl, False)
    own[...] = jnp.zeros_like(own)
    for s in range(4):
        k = 4 * y + s
        u = lax.rsqrt(jnp.dot(right_factor(rows8(vl, k)), lf[k], preferred_element_type=f32)).astype(bf16)
        own[pl.ds(pl.multiple_of(8 * k, 8), 8), :] = jnp.dot(da[k].astype(bf16), u, preferred_element_type=f32)

    kr = lax.broadcasted_iota(i32, (64, 256), 0) // 8
    kc = lax.broadcasted_iota(i32, (64, 256), 1) // 32
    mask = jnp.where(kr == kc, 1.0, 0.0)

    def far_owner(p, yy, h):
        return h * 32 + yy * 8 + p

    def far_cols(p):
        for v in range(2):
            es = [far_owner(p, yy, h) for yy in (2 * v, 2 * v + 1) for h in range(2)]
            ds = []
            for e in es:
                for k in range(2):
                    i = rem(fars[2 * k, e], 16)
                    ds.append(jnp.where(k < fcnts[0, e], da[i], 0.0))
            r = through(jnp.concatenate(ds, 0).astype(bf16), jnp.concatenate([left[e] for e in es], 0),
                        jnp.concatenate([right[e] for e in es], 0), mask).astype(bf16)
            fc[2 * v, p] = r[:32]
            fc[2 * v + 1, p] = r[32:]

    cl.wait()
    cr.wait()
    each(0, 4, far_cols)

    wait_y(igy, 0)
    own_i = pltpu.make_async_copy(igy, igot.at[row], lsem.at[0])
    own_i.start()

    def send_i(t):
        p = rem(row + 8 - t, 8)
        remote(igy, igot.at[row], s_r.at[0], r_r.at[0], (z, p // 2, rem(p, 2), y)).start()

    each(1, 8, send_i)
    each(4, 8, far_cols)
    step_y(lambda yy: fc.at[yy], fcy, 1)
    own_c = pltpu.make_async_copy(fc.at[y], fcy.at[y], lsem.at[1])
    own_c.start()

    each(1, 8, lambda t: copy_a(t, row).start())

    own_i.wait()
    wait_row(igot, 0)
    q0 = y * 8 + row
    lists = jnp.zeros((8, 128), i32)
    for s in range(32):
        lists = jnp.where(rem(lane8, 32) == s, pltpu.roll(igot[s // 4, s % 4], rem(s - q0 + 128, 128), 1), lists)
    cvm[...] = lists
    ci = pltpu.make_async_copy(cvm, csm, lsem.at[2])
    ci.start()
    for h in range(2):
        w4 = pb.at[h]
        w3 = pb.at[h, pl.ds(0, 144)]

        @pl.when(z != h * 4 + y)
        def _(w4=w4, h=h):
            remote(w4, w4, s_b, r_b.at[h], side).wait_recv()

        @pl.when(z == h * 4 + y)
        def _(w3=w3, h=h):
            remote(w3, w3, s_b, r_b.at[h], side).wait_recv()

    for h in range(2):
        feats(lambda o, h=h: pb[h, o:o + 16, :], vl, False)
        for k in range(16):
            rt[h * 16 + k] = right_factor(rows8(vl, k))
        tables(lambda o, h=h: pb[h, o:o + 16, :], db, h * 16)
    ci.wait()

    def far_col(s, h, k):
        return h * 16 + rem(csm[1 + k, 64 + h * 32 + s], 16)

    def fill_fd(p):
        for yy in range(4):
            s = p * 4 + yy
            fd[yy, p] = jnp.concatenate([db[far_col(s, h, k)] for h in range(2) for k in range(2)], 0).astype(bf16)

    each(0, 8, fill_fd)
    own_c.wait()
    own_d = pltpu.make_async_copy(fd.at[y], fdy.at[y], lsem.at[0])
    own_d.start()
    step_y(lambda yy: fd.at[yy], fdy, 2)
    own_d.wait()

    def slot_ids(b, n):
        s, h, k = 4 * b + n // 8, (n // 4) % 2, n % 4
        return (rem(csm[2 * k, h * 32 + s], 16), h * 16 + rem(csm[2 * k + 1, h * 32 + s], 16),
                k < csm[0, 64 + h * 32 + s])

    def build(b, par, first, slot):
        for g in range(16):
            i, j, _ = slot_ids(b, first + g)
            d2 = jnp.dot(rt[j], lf[par * 16 + i], preferred_element_type=f32)
            ub[slot, g] = lax.rsqrt(d2).astype(bf16)

    def apply(b, par, first, slot, rows=True, cols=True):
        for g in range(16):
            n = first + g
            i, j, _ = slot_ids(b, n)
            u = ub[slot, g]
            if rows:
                rbuf[8 * n:8 * n + 8, :] = jnp.dot(db[j].astype(bf16), u, preferred_element_type=f32)
            if cols:
                cbuf[8 * n:8 * n + 8, :] = lax.dot_general(
                    da[par * 16 + i].astype(bf16), u, (((1,), (1,)), ((), ())), preferred_element_type=f32)

    def copy_oa(b, yy, slot):
        return remote(sa.at[b, pl.ds(pl.multiple_of(yy * 32, 32), 32)], ra.at[slot], s_oa, r_oa,
                      (z, b // 2, rem(b, 2), yy))

    def row_sums(b):
        ids = [slot_ids(b, n) for n in range(32)]
        return gathered(pick_matrix([jnp.where(v[2], v[0], -1) for v in ids], 128), rbuf[...])

    def col_sums(b):
        ids = [slot_ids(b, n) for n in range(32)]
        acc_b[...] += gathered(pick_matrix([jnp.where(v[2], v[1], -1) for v in ids], 256), cbuf[...])

    def send_oa(b):
        for v in range(4):
            copy_oa(b, rem(y + v, 4), me).start()

    acc_b[...] = jnp.zeros_like(acc_b)
    build(row, 0, 0, 0)

    def group(t):
        b = rem(row + t, 8)
        nb = rem(row + t + 1, 8)
        par = rem(t, 2)
        copy_a(t + 1, nb).wait_recv()
        apply(b, par, 0, 0)
        build(b, par, 16, 1)
        prep(lambda o: pa[nb, o:o + 16, :], 1 - par)
        apply(b, par, 16, 1)
        build(nb, 1 - par, 0, 0)
        col_sums(b)
        sums = row_sums(b)

        @pl.when(t == 0)
        def _():
            own[...] += sums
            wait_y(fcy, 1)
            step_row(fcy, fcr, 1)

        @pl.when(t > 0)
        def _():
            sa[b] = sums.astype(bf16)
            send_oa(b)

        @pl.when(t == 2)
        def _():
            wait_y(fdy, 2)
            step_row(fdy, fdr, 2)

    each(0, 7, group)

    own_c2 = pltpu.make_async_copy(fcy.at[:, row], fcr.at[row], lsem.at[0])
    own_c2.start()
    own_d2 = pltpu.make_async_copy(fdy.at[:, row], fdr.at[row], lsem.at[1])
    own_d2.start()
    own_c2.wait()
    own_d2.wait()
    wait_row(fcr, 1)
    for g in range(4):
        ids = [far_col(g * 8 + n // 4, (n // 2) % 2, n % 2) for n in range(32)]
        v = jnp.concatenate([fcr[g * 2 + k // 4, k % 4] for k in range(8)], 0)
        acc_b[...] += jnp.dot(pick_matrix(ids, 256), v, preferred_element_type=f32)

    last = rem(row + 7, 8)
    apply(last, 1, 0, 0, rows=False)
    build(last, 1, 16, 1)
    apply(last, 1, 16, 1, rows=False)
    col_sums(last)
    for h in range(2):
        sb[h] = acc_b[128 * h:128 * h + 128, :].astype(bf16)

    def copy_ob(h, yy):
        return remote(sb.at[h, pl.ds(pl.multiple_of(yy * 32, 32), 32)], rb.at[z], s_ob, r_ob, (h * 4 + y, x, c, yy))

    for v in (1, 2, 3, 0):
        for h in range(2):
            if v == 0:
                @pl.when(z != h * 4 + y)
                def _(h=h):
                    copy_ob(h, y).start()
            else:
                copy_ob(h, rem(y + v, 4)).start()

    @pl.when(owner)
    def _():
        rb[z] = sb[half, quarter(32), :]

    apply(last, 1, 0, 0, cols=False)
    apply(last, 1, 16, 1, cols=False)
    sa[last] = row_sums(last).astype(bf16)
    send_oa(last)

    wait_row(fdr, 2)

    def far_rows(g):
        ids = []
        for b in range(4):
            p, yys = g * 2 + b // 2, (2 * (b % 2), 2 * (b % 2) + 1)
            es = [far_owner(p, yy, h) for yy in yys for h in range(2)]
            rbuf[64 * b:64 * b + 64, :] = through(
                jnp.concatenate([fdr[p, yy] for yy in yys], 0), jnp.concatenate([right[e] for e in es], 0),
                jnp.concatenate([left[e] for e in es], 0), mask)
            ids += [jnp.where(k < fcnts[0, e], rem(fars[2 * k, e], 16), -1) for e in es for k in range(2)]
        own[...] += gathered(pick_matrix(ids, 128), rbuf[...])

    each(0, 4, far_rows)

    sa[row] = own[...].astype(bf16)
    for v in range(1, 4):
        copy_oa(row, rem(y + v, 4), me).start()
    ra[me] = jnp.zeros((32, 256), bf16)
    part[...] = own[quarter(32), :]
    w = ra.at[pl.ds(0, 31)]
    remote(w, w, s_oa, r_oa, side).wait_recv()

    def add_a(t):
        part[...] += ((ra[4 * t].astype(f32) + ra[4 * t + 1].astype(f32))
                      + (ra[4 * t + 2].astype(f32) + ra[4 * t + 3].astype(f32)))

    each(0, 8, add_a)

    def both(f):
        @pl.when(owner)
        def _():
            f(rb.at[pl.ds(0, 7)])

        @pl.when(jnp.logical_not(owner))
        def _():
            f(rb)

    both(lambda v: remote(v, v, s_ob, r_ob, side).wait_recv())
    part[...] += (((rb[0].astype(f32) + rb[1].astype(f32)) + (rb[2].astype(f32) + rb[3].astype(f32)))
                  + ((rb[4].astype(f32) + rb[5].astype(f32)) + (rb[6].astype(f32) + rb[7].astype(f32))))

    for t in range(1, 4):
        remote(part, out.at[quarter(32)], s_o, r_o, (z, x, c, rem(y + t, 4))).start()
    out[quarter(32), :] = part[...]

    both(lambda v: remote(v, v, s_ob, r_ob, side).wait_send())
    remote(w, w, s_oa, r_oa, side).wait_send()
    w = pa.at[pl.ds(0, 7)]
    remote(w, w, s_a, r_a.at[0], side).wait_send()
    for k, (vy, vr) in enumerate(((igy, igot), (fcy, fcr), (fdy, fdr))):
        w = vy.at[pl.ds(0, 3)]
        remote(w, w, s_y.at[k], r_y.at[k], side).wait_send()
        w = vr.at[pl.ds(0, 7)]
        remote(w, w, s_r.at[k], r_r.at[k], side).wait_send()
    w = pa.at[0, pl.ds(0, 48)]
    n_b = 7

    def sent_b(t):
        remote(w, w, s_b, r_b.at[0], side).wait_send()

    each(0, n_b, sent_b)

    @pl.when(jnp.logical_not(owner))
    def _():
        sent_b(0)

    w = out.at[pl.ds(0, 96)]
    remote(w, w, s_o, r_o, side).wait_recv()
    remote(w, w, s_o, r_o, side).wait_send()


def per_device(density, positions, areas, near_pairs, near_counts, far_pairs, far_counts, far_right, far_left):
    near = near_pairs[0, 0].transpose(1, 2, 0).reshape(8, 64)
    far = far_pairs[0, 0].transpose(1, 2, 0).reshape(4, 64)
    ncnt = near_counts.reshape(1, 64)
    fcnt = far_counts.reshape(1, 64)
    left = far_left.reshape(64, 64, 256)
    right = far_right.reshape(64, 64, 256)
    vm = pl.BlockSpec(memory_space=pltpu.VMEM)
    sm = pl.BlockSpec(memory_space=pltpu.SMEM)
    hbm = pl.BlockSpec(memory_space=pl.ANY)
    V, D = pltpu.VMEM, pltpu.SemaphoreType.DMA
    out = pl.pallas_call(
        kernel,
        out_shape=jax.ShapeDtypeStruct((128, 256), f32),
        in_specs=[vm] * 6 + [sm] * 2 + [hbm] * 2,
        out_specs=vm,
        scratch_shapes=[
            V((64, 64, 256), bf16), V((64, 64, 256), bf16), V((192, 256), bf16), V((8, 192, 256), bf16),
            V((2, 192, 256), bf16), V((8, 128), i32), V((8, 128), i32), V((4, 8, 128), i32), V((8, 4, 8, 128), i32),
            V((8, 128), i32), pltpu.SMEM((8, 128), i32), V((2, 128, 128), f32), V((32, KF, 256), bf16),
            V((32, 256, KF), bf16), V((32, 8, 256), f32), V((32, 8, 256), f32),
            V((2, 16, 256, 256), bf16), V((256, 256), f32), V((256, 256), f32), V((256, 256), f32), V((128, 256), f32),
            V((4, 8, 32, 256), bf16), V((4, 8, 32, 256), bf16), V((8, 4, 32, 256), bf16),
            V((4, 8, 32, 256), bf16), V((4, 8, 32, 256), bf16), V((8, 4, 32, 256), bf16),
            V((8, 128, 256), bf16), V((2, 128, 256), bf16), V((32, 32, 256), bf16), V((8, 32, 256), bf16),
            V((32, 256), f32),
            D((3,)), D, D((8,)), D, D((2,)), D((3,)), D((3,)), D((3,)), D((3,)), D, D, D, D, D, D,
        ],
        compiler_params=pltpu.CompilerParams(collective_id=1, has_side_effects=True,
                                             vmem_limit_bytes=56 * 1024 * 1024),
    )(near, ncnt, far, density.reshape(128, 256), positions.transpose(1, 0, 2).reshape(48, 256), areas,
      far, fcnt, left, right)
    return out.reshape(16, 8, 256)


def solution(mesh):
    grid = Mesh(mesh.devices.reshape(8, 4, 2, 4), ("z", "x", "c", "y"))
    d = ("z", "x", "c")
    return jax.shard_map(
        per_device,
        mesh=grid,
        in_specs=(
            P(d, None, None),
            P(d, None, None),
            P(d, None),
            P(d, "y", None, None, None),
            P(d, "y", None),
            P(d, "y", None, None, None),
            P(d, "y", None),
            P(d, "y", None, None, None, None),
            P(d, "y", None, None, None, None),
        ),
        out_specs=P(d, None, None),
        check_vma=False,
    )
```

```python
import jax
import jax.numpy as jnp
from jax import lax
from jax.experimental import pallas as pl
from jax.experimental.pallas import tpu as pltpu
from jax.sharding import Mesh, PartitionSpec as P

f32 = jnp.float32
bf16 = jnp.bfloat16
i32 = jnp.int32
MESH = pl.DeviceIdType.MESH
KF = 48


def rem(a, n):
    return lax.rem(a, jnp.int32(n))


def plane_peer(flat):
    return flat // 8, rem(flat // 4, 2), rem(flat, 4)


def split3(v):
    h = v.astype(bf16).astype(f32)
    m = (v - h).astype(bf16).astype(f32)
    return h, m, v - h - m


def feats(load, vref, left):
    xs = [load(128 + 16 * k).astype(f32) - 0.5 for k in range(3)]
    a = load(176).astype(f32)
    w = 256.0 / (a * a)
    n = (xs[0] * xs[0] + xs[1] * xs[1] + xs[2] * xs[2] + 0.005) * w
    rows = [n, w] if left else [w, n]
    rows += [v * ((-2.0 if left else 1.0) * w) for v in xs]
    for k, r in enumerate(rows):
        vref[0, pl.ds(k, 16, stride=8), :] = r[:, :128]
        vref[1, pl.ds(k, 16, stride=8), :] = r[:, 128:]


def rows8(vref, c):
    o = pl.ds(pl.multiple_of(8 * c, 8), 8)
    return jnp.concatenate([vref[0, o, :], vref[1, o, :]], 1)


def left_factor(v):
    h, m, l = split3(v)
    return jnp.concatenate([h, h, m, m, h, l], 0).astype(bf16)


def right_factor(v):
    h, m, l = split3(v)
    return jnp.concatenate([h, m, h, m, l, h], 0).T.astype(bf16)


def through(dens, first, second, mask):
    p = lax.dot_general(dens, first, (((1,), (1,)), ((), ())), preferred_element_type=f32)
    p = (p.astype(bf16).astype(f32) * mask).astype(bf16)
    return jnp.dot(p, second, preferred_element_type=f32)


def pick_matrix(ids, rows):
    lane = lax.broadcasted_iota(i32, (1, 256), 1)
    key = jnp.full((1, 256), -8, i32)
    for n, v in enumerate(ids):
        key = jnp.where(lane // 8 == n, v * 8, key)
    key = key + rem(lane, 8)
    return jnp.where(lax.broadcasted_iota(i32, (rows, 256), 0) == key, 1.0, 0.0).astype(bf16)


def gathered(sel, v):
    hi = v.astype(bf16)
    lo = (v - hi.astype(f32)).astype(bf16)
    return jnp.dot(sel, hi, preferred_element_type=f32) + jnp.dot(sel, lo, preferred_element_type=f32)


def kernel(near, ncnt, far, dens, pos, area, fars, fcnts, left_h, right_h, out,
           left, right, pack, pa, pb, t1, t2, igy, igot, cvm, csm, vl, lf, rt, da, db, ub0, ub1, rbuf, cbuf,
           acc_b, own, fc, fcy, fcr, fd, fdy, fdr, sa, sb, ra, rb, part,
           lsem, s_a, r_a, s_b, r_b, s_y, r_y, s_r, r_r, s_oa, r_oa, s_ob, r_ob, s_o, r_o):
    z, x, c, y = (lax.axis_index(n) for n in ("z", "x", "c", "y"))
    row = x * 2 + c
    me = row * 4 + y
    half = z // 4
    zy = rem(z, 4)
    owner = zy == y

    def each(lo, hi, f):
        def body(t, _):
            f(t)
            return 0
        lax.fori_loop(lo, hi, body, 0)

    cl = pltpu.make_async_copy(left_h, left, lsem.at[0])
    cr = pltpu.make_async_copy(right_h, right, lsem.at[1])
    cl.start()
    cr.start()

    barrier = pltpu.get_barrier_semaphore()

    def greet(dev):
        pl.semaphore_signal(barrier, inc=1, device_id=dev, device_id_type=MESH)

    def plane_dev(q):
        px, pc, py = plane_peer(q)
        return (z, px, pc, py)

    each(1, 32, lambda t: greet(plane_dev(rem(me + t, 32))))
    each(1, 8, lambda t: greet((rem(z + t, 8), x, c, zy)))
    for h in range(2):
        @pl.when(z != h * 4 + y)
        def _(h=h):
            for v in range(4):
                greet((h * 4 + y, x, c, v))

    pack[0:128, :] = dens[...]
    pack[128:176, :] = pos[...]
    pack[176:192, :] = area[...]
    t1[...] = jnp.zeros_like(t1)
    t2[...] = jnp.zeros_like(t2)
    t1[:, 0:64] = near[...]
    t2[0:1, 0:64] = ncnt[...]
    t2[1:2, 0:64] = far[1:2, :]
    t2[2:3, 0:64] = far[3:4, :]
    lane8 = lax.broadcasted_iota(i32, (8, 128), 1)
    igy[y] = jnp.where(lane8 < 64, t1[...], pltpu.roll(t2[...], 64, 1))

    def quarter(n):
        return pl.ds(pl.multiple_of(y * n, n), n)

    @pl.when(owner)
    def _():
        pb[half, quarter(48), :] = pack[quarter(48), :]
        pl.semaphore_wait(barrier, 42)

    @pl.when(jnp.logical_not(owner))
    def _():
        pl.semaphore_wait(barrier, 46)

    def remote(src, dst, ss, rs, dev):
        return pltpu.make_async_remote_copy(src_ref=src, dst_ref=dst, send_sem=ss, recv_sem=rs,
                                            device_id=dev, device_id_type=MESH)

    side = (z, x, c, rem(y + 1, 4))

    def copy_b(t):
        return remote(pack.at[quarter(48)], pb.at[half, quarter(48)], s_b, r_b.at[half], (rem(z + t, 8), x, c, zy))

    for t in (4, 3, 5, 2, 6, 1, 7):
        copy_b(t).start()

    @pl.when(jnp.logical_not(owner))
    def _():
        copy_b(0).start()

    def step_y(src, dst, k):
        for t in range(1, 4):
            yy = rem(y + t, 4)
            remote(src(yy), dst.at[y], s_y.at[k], r_y.at[k], (z, x, c, yy)).start()

    def wait_y(dst, k):
        w = dst.at[pl.ds(0, 3)]
        remote(w, w, s_y.at[k], r_y.at[k], side).wait_recv()

    def step_row(src, dst, k):
        def one(t):
            p = rem(row + 8 - t, 8)
            remote(src.at[:, p], dst.at[row], s_r.at[k], r_r.at[k], (z, p // 2, rem(p, 2), y)).start()
        each(1, 8, one)

    def wait_row(dst, k):
        w = dst.at[pl.ds(0, 7)]
        remote(w, w, s_r.at[k], r_r.at[k], side).wait_recv()

    step_y(lambda yy: igy.at[y], igy, 0)

    def copy_a(t, slot):
        p = rem(row + 8 - t, 8)
        return remote(pack, pa.at[slot], s_a, r_a.at[slot], (z, p // 2, rem(p, 2), y))

    def tables(load, dref, base):
        for k in range(8):
            v = load(16 * k).astype(f32)
            dref[base + 2 * k] = v[:8]
            dref[base + 2 * k + 1] = v[8:]

    def prep(load, par):
        feats(load, vl, True)
        for k in range(16):
            lf[par * 16 + k] = left_factor(rows8(vl, k))
        tables(load, da, par * 16)

    vl[...] = jnp.zeros_like(vl)
    prep(lambda o: pack[o:o + 16, :], 0)
    feats(lambda o: pack[o:o + 16, :], vl, False)
    own[...] = jnp.zeros_like(own)
    for s in range(4):
        k = 4 * y + s
        u = lax.rsqrt(jnp.dot(right_factor(rows8(vl, k)), lf[k], preferred_element_type=f32)).astype(bf16)
        own[pl.ds(pl.multiple_of(8 * k, 8), 8), :] = jnp.dot(da[k].astype(bf16), u, preferred_element_type=f32)

    kr = lax.broadcasted_iota(i32, (64, 256), 0) // 8
    kc = lax.broadcasted_iota(i32, (64, 256), 1) // 32
    mask = jnp.where(kr == kc, 1.0, 0.0)

    def far_owner(p, yy, h):
        return h * 32 + yy * 8 + p

    def far_cols(p):
        for v in range(2):
            es = [far_owner(p, yy, h) for yy in (2 * v, 2 * v + 1) for h in range(2)]
            ds = []
            for e in es:
                for k in range(2):
                    i = rem(fars[2 * k, e], 16)
                    ds.append(jnp.where(k < fcnts[0, e], da[i], 0.0))
            r = through(jnp.concatenate(ds, 0).astype(bf16), jnp.concatenate([left[e] for e in es], 0),
                        jnp.concatenate([right[e] for e in es], 0), mask).astype(bf16)
            fc[2 * v, p] = r[:32]
            fc[2 * v + 1, p] = r[32:]

    cl.wait()
    cr.wait()
    each(0, 4, far_cols)

    wait_y(igy, 0)
    own_i = pltpu.make_async_copy(igy, igot.at[row], lsem.at[0])
    own_i.start()

    def send_i(t):
        p = rem(row + 8 - t, 8)
        remote(igy, igot.at[row], s_r.at[0], r_r.at[0], (z, p // 2, rem(p, 2), y)).start()

    each(1, 8, send_i)
    each(1, 8, lambda t: copy_a(t, row).start())
    each(4, 8, far_cols)
    step_y(lambda yy: fc.at[yy], fcy, 1)
    own_c = pltpu.make_async_copy(fc.at[y], fcy.at[y], lsem.at[1])
    own_c.start()


    own_i.wait()
    wait_row(igot, 0)
    q0 = y * 8 + row
    lists = jnp.zeros((8, 128), i32)
    for s in range(32):
        lists = jnp.where(rem(lane8, 32) == s, pltpu.roll(igot[s // 4, s % 4], rem(s - q0 + 128, 128), 1), lists)
    cvm[...] = lists
    ci = pltpu.make_async_copy(cvm, csm, lsem.at[2])
    ci.start()
    for h in range(2):
        w4 = pb.at[h]
        w3 = pb.at[h, pl.ds(0, 144)]

        @pl.when(z != h * 4 + y)
        def _(w4=w4, h=h):
            remote(w4, w4, s_b, r_b.at[h], side).wait_recv()

        @pl.when(z == h * 4 + y)
        def _(w3=w3, h=h):
            remote(w3, w3, s_b, r_b.at[h], side).wait_recv()

    for h in range(2):
        feats(lambda o, h=h: pb[h, o:o + 16, :], vl, False)
        for k in range(16):
            rt[h * 16 + k] = right_factor(rows8(vl, k))
        tables(lambda o, h=h: pb[h, o:o + 16, :], db, h * 16)
    ci.wait()

    def far_col(s, h, k):
        return h * 16 + rem(csm[1 + k, 64 + h * 32 + s], 16)

    def fill_fd(p):
        for yy in range(4):
            s = p * 4 + yy
            fd[yy, p] = jnp.concatenate([db[far_col(s, h, k)] for h in range(2) for k in range(2)], 0).astype(bf16)

    each(0, 8, fill_fd)
    own_c.wait()
    own_d = pltpu.make_async_copy(fd.at[y], fdy.at[y], lsem.at[0])
    own_d.start()
    step_y(lambda yy: fd.at[yy], fdy, 2)
    own_d.wait()

    def slot_ids(b, n):
        s, h, k = 4 * b + n // 8, (n // 4) % 2, n % 4
        return (rem(csm[2 * k, h * 32 + s], 16), h * 16 + rem(csm[2 * k + 1, h * 32 + s], 16),
                k < csm[0, 64 + h * 32 + s])

    tiles = (ub0, ub1)

    def build(b, par, n):
        i, j, _ = slot_ids(b, n)
        d2 = jnp.dot(rt[j], lf[par * 16 + i], preferred_element_type=f32)
        tiles[n // 16][n % 16] = lax.rsqrt(d2).astype(bf16)

    def apply(b, par, n, rows=True, cols=True):
        i, j, _ = slot_ids(b, n)
        u = tiles[n // 16][n % 16]
        if rows:
            rbuf[8 * n:8 * n + 8, :] = jnp.dot(db[j].astype(bf16), u, preferred_element_type=f32)
        if cols:
            cbuf[8 * n:8 * n + 8, :] = lax.dot_general(
                da[par * 16 + i].astype(bf16), u, (((1,), (1,)), ((), ())), preferred_element_type=f32)

    def copy_oa(b, yy, slot):
        return remote(sa.at[b, pl.ds(pl.multiple_of(yy * 32, 32), 32)], ra.at[slot], s_oa, r_oa,
                      (z, b // 2, rem(b, 2), yy))

    def row_sums(b):
        ids = [slot_ids(b, n) for n in range(32)]
        return gathered(pick_matrix([jnp.where(v[2], v[0], -1) for v in ids], 128), rbuf[...])

    def col_sums(b):
        ids = [slot_ids(b, n) for n in range(32)]
        acc_b[...] += gathered(pick_matrix([jnp.where(v[2], v[1], -1) for v in ids], 256), cbuf[...])

    def send_oa(b):
        for v in range(4):
            copy_oa(b, rem(y + v, 4), me).start()

    acc_b[...] = jnp.zeros_like(acc_b)
    for n in range(16):
        build(row, 0, n)

    def group(t):
        b = rem(row + t, 8)
        nb = rem(row + t + 1, 8)
        par = rem(t, 2)
        copy_a(t + 1, nb).wait_recv()
        for n in range(16):
            apply(b, par, n)
            build(b, par, 16 + n)
        prep(lambda o: pa[nb, o:o + 16, :], 1 - par)
        for n in range(16):
            apply(b, par, 16 + n)
            build(nb, 1 - par, n)
        col_sums(b)
        sums = row_sums(b)

        @pl.when(t == 0)
        def _():
            own[...] += sums
            wait_y(fcy, 1)
            step_row(fcy, fcr, 1)

        @pl.when(t > 0)
        def _():
            sa[b] = sums.astype(bf16)
            send_oa(b)

        @pl.when(t == 2)
        def _():
            wait_y(fdy, 2)
            step_row(fdy, fdr, 2)

    each(0, 7, group)

    own_c2 = pltpu.make_async_copy(fcy.at[:, row], fcr.at[row], lsem.at[0])
    own_c2.start()
    own_d2 = pltpu.make_async_copy(fdy.at[:, row], fdr.at[row], lsem.at[1])
    own_d2.start()
    own_c2.wait()
    own_d2.wait()
    wait_row(fcr, 1)
    for g in range(4):
        ids = [far_col(g * 8 + n // 4, (n // 2) % 2, n % 2) for n in range(32)]
        v = jnp.concatenate([fcr[g * 2 + k // 4, k % 4] for k in range(8)], 0)
        acc_b[...] += jnp.dot(pick_matrix(ids, 256), v, preferred_element_type=f32)

    last = rem(row + 7, 8)
    for n in range(16):
        apply(last, 1, n, rows=False)
        build(last, 1, 16 + n)
    for n in range(16):
        apply(last, 1, 16 + n, rows=False)
    col_sums(last)
    for h in range(2):
        sb[h] = acc_b[128 * h:128 * h + 128, :].astype(bf16)

    def copy_ob(h, yy):
        return remote(sb.at[h, pl.ds(pl.multiple_of(yy * 32, 32), 32)], rb.at[z], s_ob, r_ob, (h * 4 + y, x, c, yy))

    for v in (1, 2, 3, 0):
        for h in range(2):
            if v == 0:
                @pl.when(z != h * 4 + y)
                def _(h=h):
                    copy_ob(h, y).start()
            else:
                copy_ob(h, rem(y + v, 4)).start()

    @pl.when(owner)
    def _():
        rb[z] = sb[half, quarter(32), :]

    for n in range(32):
        apply(last, 1, n, cols=False)
    sa[last] = row_sums(last).astype(bf16)
    send_oa(last)

    wait_row(fdr, 2)

    def far_rows(g):
        ids = []
        for b in range(4):
            p, yys = g * 2 + b // 2, (2 * (b % 2), 2 * (b % 2) + 1)
            es = [far_owner(p, yy, h) for yy in yys for h in range(2)]
            rbuf[64 * b:64 * b + 64, :] = through(
                jnp.concatenate([fdr[p, yy] for yy in yys], 0), jnp.concatenate([right[e] for e in es], 0),
                jnp.concatenate([left[e] for e in es], 0), mask)
            ids += [jnp.where(k < fcnts[0, e], rem(fars[2 * k, e], 16), -1) for e in es for k in range(2)]
        own[...] += gathered(pick_matrix(ids, 128), rbuf[...])

    each(0, 4, far_rows)

    sa[row] = own[...].astype(bf16)
    for v in range(1, 4):
        copy_oa(row, rem(y + v, 4), me).start()
    ra[me] = jnp.zeros((32, 256), bf16)
    part[...] = own[quarter(32), :]
    w = ra.at[pl.ds(0, 31)]
    remote(w, w, s_oa, r_oa, side).wait_recv()

    def add_a(t):
        part[...] += ((ra[4 * t].astype(f32) + ra[4 * t + 1].astype(f32))
                      + (ra[4 * t + 2].astype(f32) + ra[4 * t + 3].astype(f32)))

    each(0, 8, add_a)

    def both(f):
        @pl.when(owner)
        def _():
            f(rb.at[pl.ds(0, 7)])

        @pl.when(jnp.logical_not(owner))
        def _():
            f(rb)

    both(lambda v: remote(v, v, s_ob, r_ob, side).wait_recv())
    part[...] += (((rb[0].astype(f32) + rb[1].astype(f32)) + (rb[2].astype(f32) + rb[3].astype(f32)))
                  + ((rb[4].astype(f32) + rb[5].astype(f32)) + (rb[6].astype(f32) + rb[7].astype(f32))))

    for t in range(1, 4):
        remote(part, out.at[quarter(32)], s_o, r_o, (z, x, c, rem(y + t, 4))).start()
    out[quarter(32), :] = part[...]

    both(lambda v: remote(v, v, s_ob, r_ob, side).wait_send())
    remote(w, w, s_oa, r_oa, side).wait_send()
    w = pa.at[pl.ds(0, 7)]
    remote(w, w, s_a, r_a.at[0], side).wait_send()
    for k, (vy, vr) in enumerate(((igy, igot), (fcy, fcr), (fdy, fdr))):
        w = vy.at[pl.ds(0, 3)]
        remote(w, w, s_y.at[k], r_y.at[k], side).wait_send()
        w = vr.at[pl.ds(0, 7)]
        remote(w, w, s_r.at[k], r_r.at[k], side).wait_send()
    w = pa.at[0, pl.ds(0, 48)]
    n_b = 7

    def sent_b(t):
        remote(w, w, s_b, r_b.at[0], side).wait_send()

    each(0, n_b, sent_b)

    @pl.when(jnp.logical_not(owner))
    def _():
        sent_b(0)

    w = out.at[pl.ds(0, 96)]
    remote(w, w, s_o, r_o, side).wait_recv()
    remote(w, w, s_o, r_o, side).wait_send()


def per_device(density, positions, areas, near_pairs, near_counts, far_pairs, far_counts, far_right, far_left):
    near = near_pairs[0, 0].transpose(1, 2, 0).reshape(8, 64)
    far = far_pairs[0, 0].transpose(1, 2, 0).reshape(4, 64)
    ncnt = near_counts.reshape(1, 64)
    fcnt = far_counts.reshape(1, 64)
    left = far_left.reshape(64, 64, 256)
    right = far_right.reshape(64, 64, 256)
    vm = pl.BlockSpec(memory_space=pltpu.VMEM)
    sm = pl.BlockSpec(memory_space=pltpu.SMEM)
    hbm = pl.BlockSpec(memory_space=pl.ANY)
    V, D = pltpu.VMEM, pltpu.SemaphoreType.DMA
    out = pl.pallas_call(
        kernel,
        out_shape=jax.ShapeDtypeStruct((128, 256), f32),
        in_specs=[vm] * 6 + [sm] * 2 + [hbm] * 2,
        out_specs=vm,
        scratch_shapes=[
            V((64, 64, 256), bf16), V((64, 64, 256), bf16), V((192, 256), bf16), V((8, 192, 256), bf16),
            V((2, 192, 256), bf16), V((8, 128), i32), V((8, 128), i32), V((4, 8, 128), i32), V((8, 4, 8, 128), i32),
            V((8, 128), i32), pltpu.SMEM((8, 128), i32), V((2, 128, 128), f32), V((32, KF, 256), bf16),
            V((32, 256, KF), bf16), V((32, 8, 256), f32), V((32, 8, 256), f32),
            V((16, 256, 256), bf16), V((16, 256, 256), bf16), V((256, 256), f32), V((256, 256), f32), V((256, 256), f32), V((128, 256), f32),
            V((4, 8, 32, 256), bf16), V((4, 8, 32, 256), bf16), V((8, 4, 32, 256), bf16),
            V((4, 8, 32, 256), bf16), V((4, 8, 32, 256), bf16), V((8, 4, 32, 256), bf16),
            V((8, 128, 256), bf16), V((2, 128, 256), bf16), V((32, 32, 256), bf16), V((8, 32, 256), bf16),
            V((32, 256), f32),
            D((3,)), D, D((8,)), D, D((2,)), D((3,)), D((3,)), D((3,)), D((3,)), D, D, D, D, D, D,
        ],
        compiler_params=pltpu.CompilerParams(collective_id=1, has_side_effects=True,
                                             vmem_limit_bytes=56 * 1024 * 1024),
    )(near, ncnt, far, density.reshape(128, 256), positions.transpose(1, 0, 2).reshape(48, 256), areas,
      far, fcnt, left, right)
    return out.reshape(16, 8, 256)


def solution(mesh):
    grid = Mesh(mesh.devices.reshape(8, 4, 2, 4), ("z", "x", "c", "y"))
    d = ("z", "x", "c")
    return jax.shard_map(
        per_device,
        mesh=grid,
        in_specs=(
            P(d, None, None),
            P(d, None, None),
            P(d, None),
            P(d, "y", None, None, None),
            P(d, "y", None),
            P(d, "y", None, None, None),
            P(d, "y", None),
            P(d, "y", None, None, None, None),
            P(d, "y", None, None, None, None),
        ),
        out_specs=P(d, None, None),
        check_vma=False,
    )
```

```python
import jax
import jax.numpy as jnp
from jax import lax
from jax.experimental import pallas as pl
from jax.experimental.pallas import tpu as pltpu
from jax.sharding import Mesh, PartitionSpec as P

f32 = jnp.float32
bf16 = jnp.bfloat16
i32 = jnp.int32
MESH = pl.DeviceIdType.MESH
KF = 48


def rem(a, n):
    return lax.rem(a, jnp.int32(n))


def plane_peer(flat):
    return flat // 8, rem(flat // 4, 2), rem(flat, 4)


def split3(v):
    h = v.astype(bf16).astype(f32)
    m = (v - h).astype(bf16).astype(f32)
    return h, m, v - h - m


def feats(load, vref, left):
    xs = [load(128 + 16 * k).astype(f32) - 0.5 for k in range(3)]
    a = load(176).astype(f32)
    w = 256.0 / (a * a)
    n = (xs[0] * xs[0] + xs[1] * xs[1] + xs[2] * xs[2] + 0.005) * w
    rows = [n, w] if left else [w, n]
    rows += [v * ((-2.0 if left else 1.0) * w) for v in xs]
    for k, r in enumerate(rows):
        vref[0, pl.ds(k, 16, stride=8), :] = r[:, :128]
        vref[1, pl.ds(k, 16, stride=8), :] = r[:, 128:]


def rows8(vref, c):
    o = pl.ds(pl.multiple_of(8 * c, 8), 8)
    return jnp.concatenate([vref[0, o, :], vref[1, o, :]], 1)


def left_factor(v):
    h, m, l = split3(v)
    return jnp.concatenate([h, h, m, m, h, l], 0).astype(bf16)


def right_factor(v):
    h, m, l = split3(v)
    return jnp.concatenate([h, m, h, m, l, h], 0).T.astype(bf16)


def through(dens, first, second, mask):
    p = lax.dot_general(dens, first, (((1,), (1,)), ((), ())), preferred_element_type=f32)
    p = (p.astype(bf16).astype(f32) * mask).astype(bf16)
    return jnp.dot(p, second, preferred_element_type=f32)


def pick_matrix(ids, rows):
    lane = lax.broadcasted_iota(i32, (1, 256), 1)
    key = jnp.full((1, 256), -8, i32)
    for n, v in enumerate(ids):
        key = jnp.where(lane // 8 == n, v * 8, key)
    key = key + rem(lane, 8)
    return jnp.where(lax.broadcasted_iota(i32, (rows, 256), 0) == key, 1.0, 0.0).astype(bf16)


def gathered(sel, v):
    hi = v.astype(bf16)
    lo = (v - hi.astype(f32)).astype(bf16)
    return jnp.dot(sel, hi, preferred_element_type=f32) + jnp.dot(sel, lo, preferred_element_type=f32)


def kernel(near, ncnt, far, dens, pos, area, fars, fcnts, left_h, right_h, out,
           left, right, pack, pa, pb, t1, t2, igy, igot, cvm, csm, vl, lf, rt, da, db, ub0, ub1, rbuf, cbuf,
           acc_b, own, fc, fcy, fcr, fd, fdy, fdr, sa, sb, ra, rb, part,
           lsem, s_a, r_a, s_b, r_b, s_y, r_y, s_r, r_r, s_oa, r_oa, s_ob, r_ob, s_o, r_o):
    z, x, c, y = (lax.axis_index(n) for n in ("z", "x", "c", "y"))
    row = x * 2 + c
    me = row * 4 + y
    half = z // 4
    zy = rem(z, 4)
    owner = zy == y

    def each(lo, hi, f):
        def body(t, _):
            f(t)
            return 0
        lax.fori_loop(lo, hi, body, 0)

    cl = pltpu.make_async_copy(left_h, left, lsem.at[0])
    cr = pltpu.make_async_copy(right_h, right, lsem.at[1])
    cl.start()
    cr.start()

    barrier = pltpu.get_barrier_semaphore()

    def greet(dev):
        pl.semaphore_signal(barrier, inc=1, device_id=dev, device_id_type=MESH)

    def plane_dev(q):
        px, pc, py = plane_peer(q)
        return (z, px, pc, py)

    each(1, 32, lambda t: greet(plane_dev(rem(me + t, 32))))
    each(1, 8, lambda t: greet((rem(z + t, 8), x, c, zy)))
    for h in range(2):
        @pl.when(z != h * 4 + y)
        def _(h=h):
            for v in range(4):
                greet((h * 4 + y, x, c, v))

    pack[0:128, :] = dens[...]
    pack[128:176, :] = pos[...]
    pack[176:192, :] = area[...]
    t1[...] = jnp.zeros_like(t1)
    t2[...] = jnp.zeros_like(t2)
    t1[:, 0:64] = near[...]
    t2[0:1, 0:64] = ncnt[...]
    t2[1:2, 0:64] = far[1:2, :]
    t2[2:3, 0:64] = far[3:4, :]
    lane8 = lax.broadcasted_iota(i32, (8, 128), 1)
    igy[y] = jnp.where(lane8 < 64, t1[...], pltpu.roll(t2[...], 64, 1))

    def quarter(n):
        return pl.ds(pl.multiple_of(y * n, n), n)

    @pl.when(owner)
    def _():
        pb[half, quarter(48), :] = pack[quarter(48), :]
        pl.semaphore_wait(barrier, 42)

    @pl.when(jnp.logical_not(owner))
    def _():
        pl.semaphore_wait(barrier, 46)

    def remote(src, dst, ss, rs, dev):
        return pltpu.make_async_remote_copy(src_ref=src, dst_ref=dst, send_sem=ss, recv_sem=rs,
                                            device_id=dev, device_id_type=MESH)

    side = (z, x, c, rem(y + 1, 4))

    def copy_b(t):
        return remote(pack.at[quarter(48)], pb.at[half, quarter(48)], s_b, r_b.at[half], (rem(z + t, 8), x, c, zy))

    for t in (4, 3, 5, 2, 6, 1, 7):
        copy_b(t).start()

    @pl.when(jnp.logical_not(owner))
    def _():
        copy_b(0).start()

    def step_y(src, dst, k):
        for t in range(1, 4):
            yy = rem(y + t, 4)
            remote(src(yy), dst.at[y], s_y.at[k], r_y.at[k], (z, x, c, yy)).start()

    def wait_y(dst, k):
        w = dst.at[pl.ds(0, 3)]
        remote(w, w, s_y.at[k], r_y.at[k], side).wait_recv()

    def step_row(src, dst, k):
        def one(t):
            p = rem(row + 8 - t, 8)
            remote(src.at[:, p], dst.at[row], s_r.at[k], r_r.at[k], (z, p // 2, rem(p, 2), y)).start()
        each(1, 8, one)

    def wait_row(dst, k):
        w = dst.at[pl.ds(0, 7)]
        remote(w, w, s_r.at[k], r_r.at[k], side).wait_recv()

    step_y(lambda yy: igy.at[y], igy, 0)

    def copy_a(t, slot):
        p = rem(row + 8 - t, 8)
        return remote(pack, pa.at[slot], s_a, r_a.at[slot], (z, p // 2, rem(p, 2), y))

    def tables(load, dref, base):
        for k in range(8):
            v = load(16 * k).astype(f32)
            dref[base + 2 * k] = v[:8]
            dref[base + 2 * k + 1] = v[8:]

    def prep(load, par):
        feats(load, vl, True)
        for k in range(16):
            lf[par * 16 + k] = left_factor(rows8(vl, k))
        tables(load, da, par * 16)

    vl[...] = jnp.zeros_like(vl)
    prep(lambda o: pack[o:o + 16, :], 0)
    feats(lambda o: pack[o:o + 16, :], vl, False)
    own[...] = jnp.zeros_like(own)
    for s in range(4):
        k = 4 * y + s
        u = lax.rsqrt(jnp.dot(right_factor(rows8(vl, k)), lf[k], preferred_element_type=f32)).astype(bf16)
        own[pl.ds(pl.multiple_of(8 * k, 8), 8), :] = jnp.dot(da[k].astype(bf16), u, preferred_element_type=f32)

    kr = lax.broadcasted_iota(i32, (64, 256), 0) // 8
    kc = lax.broadcasted_iota(i32, (64, 256), 1) // 32
    mask = jnp.where(kr == kc, 1.0, 0.0)

    def far_owner(p, yy, h):
        return h * 32 + yy * 8 + p

    def far_cols(p):
        for v in range(2):
            es = [far_owner(p, yy, h) for yy in (2 * v, 2 * v + 1) for h in range(2)]
            ds = []
            for e in es:
                for k in range(2):
                    i = rem(fars[2 * k, e], 16)
                    ds.append(jnp.where(k < fcnts[0, e], da[i], 0.0))
            r = through(jnp.concatenate(ds, 0).astype(bf16), jnp.concatenate([left[e] for e in es], 0),
                        jnp.concatenate([right[e] for e in es], 0), mask).astype(bf16)
            fc[2 * v, p] = r[:32]
            fc[2 * v + 1, p] = r[32:]

    cl.wait()
    cr.wait()
    each(0, 4, far_cols)

    wait_y(igy, 0)
    own_i = pltpu.make_async_copy(igy, igot.at[row], lsem.at[0])
    own_i.start()

    def send_i(t):
        p = rem(row + 8 - t, 8)
        remote(igy, igot.at[row], s_r.at[0], r_r.at[0], (z, p // 2, rem(p, 2), y)).start()

    each(1, 8, send_i)
    each(1, 8, lambda t: copy_a(t, row).start())
    each(4, 8, far_cols)
    step_y(lambda yy: fc.at[yy], fcy, 1)
    own_c = pltpu.make_async_copy(fc.at[y], fcy.at[y], lsem.at[1])
    own_c.start()


    own_i.wait()
    wait_row(igot, 0)
    q0 = y * 8 + row
    lists = jnp.zeros((8, 128), i32)
    for s in range(32):
        lists = jnp.where(rem(lane8, 32) == s, pltpu.roll(igot[s // 4, s % 4], rem(s - q0 + 128, 128), 1), lists)
    cvm[...] = lists
    ci = pltpu.make_async_copy(cvm, csm, lsem.at[2])
    ci.start()
    for h in range(2):
        w4 = pb.at[h]
        w3 = pb.at[h, pl.ds(0, 144)]

        @pl.when(z != h * 4 + y)
        def _(w4=w4, h=h):
            remote(w4, w4, s_b, r_b.at[h], side).wait_recv()

        @pl.when(z == h * 4 + y)
        def _(w3=w3, h=h):
            remote(w3, w3, s_b, r_b.at[h], side).wait_recv()

    for h in range(2):
        feats(lambda o, h=h: pb[h, o:o + 16, :], vl, False)
        for k in range(16):
            rt[h * 16 + k] = right_factor(rows8(vl, k))
        tables(lambda o, h=h: pb[h, o:o + 16, :], db, h * 16)
    ci.wait()

    def far_col(s, h, k):
        return h * 16 + rem(csm[1 + k, 64 + h * 32 + s], 16)

    def fill_fd(p):
        for yy in range(4):
            s = p * 4 + yy
            fd[yy, p] = jnp.concatenate([db[far_col(s, h, k)] for h in range(2) for k in range(2)], 0).astype(bf16)

    each(0, 8, fill_fd)
    own_c.wait()
    own_d = pltpu.make_async_copy(fd.at[y], fdy.at[y], lsem.at[0])
    own_d.start()
    step_y(lambda yy: fd.at[yy], fdy, 2)
    own_d.wait()

    def slot_ids(b, n):
        s, h, k = 4 * b + n // 8, (n // 4) % 2, n % 4
        return (rem(csm[2 * k, h * 32 + s], 16), h * 16 + rem(csm[2 * k + 1, h * 32 + s], 16),
                k < csm[0, 64 + h * 32 + s])

    tiles = (ub0, ub1)

    def build(b, par, n):
        i, j, _ = slot_ids(b, n)
        d2 = jnp.dot(rt[j], lf[par * 16 + i], preferred_element_type=f32)
        tiles[n // 16][n % 16] = lax.rsqrt(d2).astype(bf16)

    def apply(b, par, n, rows=True, cols=True):
        i, j, _ = slot_ids(b, n)
        u = tiles[n // 16][n % 16]
        if rows:
            rbuf[8 * n:8 * n + 8, :] = jnp.dot(db[j].astype(bf16), u, preferred_element_type=f32)
        if cols:
            cbuf[8 * n:8 * n + 8, :] = lax.dot_general(
                da[par * 16 + i].astype(bf16), u, (((1,), (1,)), ((), ())), preferred_element_type=f32)

    def copy_oa(b, yy, slot):
        return remote(sa.at[b, pl.ds(pl.multiple_of(yy * 32, 32), 32)], ra.at[slot], s_oa, r_oa,
                      (z, b // 2, rem(b, 2), yy))

    def row_sums(b):
        ids = [slot_ids(b, n) for n in range(32)]
        return gathered(pick_matrix([jnp.where(v[2], v[0], -1) for v in ids], 128), rbuf[...])

    def col_sums(b):
        ids = [slot_ids(b, n) for n in range(32)]
        acc_b[...] += gathered(pick_matrix([jnp.where(v[2], v[1], -1) for v in ids], 256), cbuf[...])

    def send_oa(b):
        for v in range(4):
            copy_oa(b, rem(y + v, 4), me).start()

    acc_b[...] = jnp.zeros_like(acc_b)
    for n in range(16):
        build(row, 0, n)

    def group(t):
        b = rem(row + t, 8)
        nb = rem(row + t + 1, 8)
        par = rem(t, 2)
        copy_a(t + 1, nb).wait_recv()
        for n in range(16):
            apply(b, par, n)
            build(b, par, 16 + n)
        prep(lambda o: pa[nb, o:o + 16, :], 1 - par)
        for n in range(16):
            apply(b, par, 16 + n)
            build(nb, 1 - par, n)
        col_sums(b)
        sums = row_sums(b)

        @pl.when(t == 0)
        def _():
            own[...] += sums

        @pl.when(t > 0)
        def _():
            sa[b] = sums.astype(bf16)
            send_oa(b)

        @pl.when(t == 1)
        def _():
            wait_y(fcy, 1)
            step_row(fcy, fcr, 1)

        @pl.when(t == 3)
        def _():
            wait_y(fdy, 2)
            step_row(fdy, fdr, 2)

    each(0, 7, group)

    own_c2 = pltpu.make_async_copy(fcy.at[:, row], fcr.at[row], lsem.at[0])
    own_c2.start()
    own_d2 = pltpu.make_async_copy(fdy.at[:, row], fdr.at[row], lsem.at[1])
    own_d2.start()
    own_c2.wait()
    own_d2.wait()
    wait_row(fcr, 1)
    for g in range(4):
        ids = [far_col(g * 8 + n // 4, (n // 2) % 2, n % 2) for n in range(32)]
        v = jnp.concatenate([fcr[g * 2 + k // 4, k % 4] for k in range(8)], 0)
        acc_b[...] += jnp.dot(pick_matrix(ids, 256), v, preferred_element_type=f32)

    last = rem(row + 7, 8)
    for n in range(16):
        apply(last, 1, n, rows=False)
        build(last, 1, 16 + n)
    for n in range(16):
        apply(last, 1, 16 + n, rows=False)
    col_sums(last)
    for h in range(2):
        sb[h] = acc_b[128 * h:128 * h + 128, :].astype(bf16)

    def copy_ob(h, yy):
        return remote(sb.at[h, pl.ds(pl.multiple_of(yy * 32, 32), 32)], rb.at[z], s_ob, r_ob, (h * 4 + y, x, c, yy))

    for v in (1, 2, 3, 0):
        for h in range(2):
            if v == 0:
                @pl.when(z != h * 4 + y)
                def _(h=h):
                    copy_ob(h, y).start()
            else:
                copy_ob(h, rem(y + v, 4)).start()

    @pl.when(owner)
    def _():
        rb[z] = sb[half, quarter(32), :]

    for n in range(32):
        apply(last, 1, n, cols=False)
    sa[last] = row_sums(last).astype(bf16)
    send_oa(last)

    wait_row(fdr, 2)

    def far_rows(g):
        buf = (rbuf, cbuf)[g % 2]
        ids = []
        for b in range(4):
            p, yys = g * 2 + b // 2, (2 * (b % 2), 2 * (b % 2) + 1)
            es = [far_owner(p, yy, h) for yy in yys for h in range(2)]
            buf[64 * b:64 * b + 64, :] = through(
                jnp.concatenate([fdr[p, yy] for yy in yys], 0), jnp.concatenate([right[e] for e in es], 0),
                jnp.concatenate([left[e] for e in es], 0), mask)
            ids += [jnp.where(k < fcnts[0, e], rem(fars[2 * k, e], 16), -1) for e in es for k in range(2)]
        return gathered(pick_matrix(ids, 128), buf[...])

    own[...] += (far_rows(0) + far_rows(1)) + (far_rows(2) + far_rows(3))

    sa[row] = own[...].astype(bf16)
    for v in range(1, 4):
        copy_oa(row, rem(y + v, 4), me).start()
    ra[me] = jnp.zeros((32, 256), bf16)
    part[...] = own[quarter(32), :]
    w = ra.at[pl.ds(0, 31)]
    remote(w, w, s_oa, r_oa, side).wait_recv()

    def add_a(t):
        part[...] += ((ra[4 * t].astype(f32) + ra[4 * t + 1].astype(f32))
                      + (ra[4 * t + 2].astype(f32) + ra[4 * t + 3].astype(f32)))

    each(0, 8, add_a)

    def both(f):
        @pl.when(owner)
        def _():
            f(rb.at[pl.ds(0, 7)])

        @pl.when(jnp.logical_not(owner))
        def _():
            f(rb)

    both(lambda v: remote(v, v, s_ob, r_ob, side).wait_recv())
    part[...] += (((rb[0].astype(f32) + rb[1].astype(f32)) + (rb[2].astype(f32) + rb[3].astype(f32)))
                  + ((rb[4].astype(f32) + rb[5].astype(f32)) + (rb[6].astype(f32) + rb[7].astype(f32))))

    for t in range(1, 4):
        remote(part, out.at[quarter(32)], s_o, r_o, (z, x, c, rem(y + t, 4))).start()
    out[quarter(32), :] = part[...]

    both(lambda v: remote(v, v, s_ob, r_ob, side).wait_send())
    remote(w, w, s_oa, r_oa, side).wait_send()
    w = pa.at[pl.ds(0, 7)]
    remote(w, w, s_a, r_a.at[0], side).wait_send()
    for k, (vy, vr) in enumerate(((igy, igot), (fcy, fcr), (fdy, fdr))):
        w = vy.at[pl.ds(0, 3)]
        remote(w, w, s_y.at[k], r_y.at[k], side).wait_send()
        w = vr.at[pl.ds(0, 7)]
        remote(w, w, s_r.at[k], r_r.at[k], side).wait_send()
    w = pa.at[0, pl.ds(0, 48)]
    n_b = 7

    def sent_b(t):
        remote(w, w, s_b, r_b.at[0], side).wait_send()

    each(0, n_b, sent_b)

    @pl.when(jnp.logical_not(owner))
    def _():
        sent_b(0)

    w = out.at[pl.ds(0, 96)]
    remote(w, w, s_o, r_o, side).wait_recv()
    remote(w, w, s_o, r_o, side).wait_send()


def per_device(density, positions, areas, near_pairs, near_counts, far_pairs, far_counts, far_right, far_left):
    near = near_pairs[0, 0].transpose(1, 2, 0).reshape(8, 64)
    far = far_pairs[0, 0].transpose(1, 2, 0).reshape(4, 64)
    ncnt = near_counts.reshape(1, 64)
    fcnt = far_counts.reshape(1, 64)
    left = far_left.reshape(64, 64, 256)
    right = far_right.reshape(64, 64, 256)
    vm = pl.BlockSpec(memory_space=pltpu.VMEM)
    sm = pl.BlockSpec(memory_space=pltpu.SMEM)
    hbm = pl.BlockSpec(memory_space=pl.ANY)
    V, D = pltpu.VMEM, pltpu.SemaphoreType.DMA
    out = pl.pallas_call(
        kernel,
        out_shape=jax.ShapeDtypeStruct((128, 256), f32),
        in_specs=[vm] * 6 + [sm] * 2 + [hbm] * 2,
        out_specs=vm,
        scratch_shapes=[
            V((64, 64, 256), bf16), V((64, 64, 256), bf16), V((192, 256), bf16), V((8, 192, 256), bf16),
            V((2, 192, 256), bf16), V((8, 128), i32), V((8, 128), i32), V((4, 8, 128), i32), V((8, 4, 8, 128), i32),
            V((8, 128), i32), pltpu.SMEM((8, 128), i32), V((2, 128, 128), f32), V((32, KF, 256), bf16),
            V((32, 256, KF), bf16), V((32, 8, 256), f32), V((32, 8, 256), f32),
            V((16, 256, 256), bf16), V((16, 256, 256), bf16), V((256, 256), f32), V((256, 256), f32), V((256, 256), f32), V((128, 256), f32),
            V((4, 8, 32, 256), bf16), V((4, 8, 32, 256), bf16), V((8, 4, 32, 256), bf16),
            V((4, 8, 32, 256), bf16), V((4, 8, 32, 256), bf16), V((8, 4, 32, 256), bf16),
            V((8, 128, 256), bf16), V((2, 128, 256), bf16), V((32, 32, 256), bf16), V((8, 32, 256), bf16),
            V((32, 256), f32),
            D((3,)), D, D((8,)), D, D((2,)), D((3,)), D((3,)), D((3,)), D((3,)), D, D, D, D, D, D,
        ],
        compiler_params=pltpu.CompilerParams(collective_id=1, has_side_effects=True,
                                             vmem_limit_bytes=56 * 1024 * 1024),
    )(near, ncnt, far, density.reshape(128, 256), positions.transpose(1, 0, 2).reshape(48, 256), areas,
      far, fcnt, left, right)
    return out.reshape(16, 8, 256)


def solution(mesh):
    grid = Mesh(mesh.devices.reshape(8, 4, 2, 4), ("z", "x", "c", "y"))
    d = ("z", "x", "c")
    return jax.shard_map(
        per_device,
        mesh=grid,
        in_specs=(
            P(d, None, None),
            P(d, None, None),
            P(d, None),
            P(d, "y", None, None, None),
            P(d, "y", None),
            P(d, "y", None, None, None),
            P(d, "y", None),
            P(d, "y", None, None, None, None),
            P(d, "y", None, None, None, None),
        ),
        out_specs=P(d, None, None),
        check_vma=False,
    )
```

```python
import jax
import jax.numpy as jnp
from jax import lax
from jax.experimental import pallas as pl
from jax.experimental.pallas import tpu as pltpu
from jax.sharding import Mesh, PartitionSpec as P

f32 = jnp.float32
bf16 = jnp.bfloat16
i32 = jnp.int32
MESH = pl.DeviceIdType.MESH
KF = 48


def rem(a, n):
    return lax.rem(a, jnp.int32(n))


def plane_peer(flat):
    return flat // 8, rem(flat // 4, 2), rem(flat, 4)


def split3(v):
    h = v.astype(bf16).astype(f32)
    m = (v - h).astype(bf16).astype(f32)
    return h, m, v - h - m


def feats(load, vref, left):
    xs = [load(128 + 16 * k).astype(f32) - 0.5 for k in range(3)]
    a = load(176).astype(f32)
    w = 256.0 / (a * a)
    n = (xs[0] * xs[0] + xs[1] * xs[1] + xs[2] * xs[2] + 0.005) * w
    rows = [n, w] if left else [w, n]
    rows += [v * ((-2.0 if left else 1.0) * w) for v in xs]
    for k, r in enumerate(rows):
        vref[0, pl.ds(k, 16, stride=8), :] = r[:, :128]
        vref[1, pl.ds(k, 16, stride=8), :] = r[:, 128:]


def rows8(vref, c):
    o = pl.ds(pl.multiple_of(8 * c, 8), 8)
    return jnp.concatenate([vref[0, o, :], vref[1, o, :]], 1)


def left_factor(v):
    h, m, l = split3(v)
    return jnp.concatenate([h, h, m, m, h, l], 0).astype(bf16)


def right_factor(v):
    h, m, l = split3(v)
    return jnp.concatenate([h, m, h, m, l, h], 0).T.astype(bf16)


def through(dens, first, second, mask):
    p = lax.dot_general(dens, first, (((1,), (1,)), ((), ())), preferred_element_type=f32)
    p = (p.astype(bf16).astype(f32) * mask).astype(bf16)
    return jnp.dot(p, second, preferred_element_type=f32)


def pick_matrix(ids, rows):
    lane = lax.broadcasted_iota(i32, (1, 256), 1)
    key = jnp.full((1, 256), -8, i32)
    for n, v in enumerate(ids):
        key = jnp.where(lane // 8 == n, v * 8, key)
    key = key + rem(lane, 8)
    return jnp.where(lax.broadcasted_iota(i32, (rows, 256), 0) == key, 1.0, 0.0).astype(bf16)


def gathered(sel, v):
    hi = v.astype(bf16)
    lo = (v - hi.astype(f32)).astype(bf16)
    return jnp.dot(sel, hi, preferred_element_type=f32) + jnp.dot(sel, lo, preferred_element_type=f32)


def kernel(near, ncnt, far, dens, pos, area, fars, fcnts, left_h, right_h, out,
           left, right, pack, pa, pb, t1, t2, igy, igot, cvm, csm, vl, lf, rt, da, db, ub0, ub1, rbuf, cbuf,
           acc_b, own, fc, fcy, fcr, fd, fdy, fdr, sa, sb, ra, rb, part,
           lsem, s_a, r_a, s_b, r_b, s_y, r_y, s_r, r_r, s_oa, r_oa, s_ob, r_ob, s_o, r_o):
    z, x, c, y = (lax.axis_index(n) for n in ("z", "x", "c", "y"))
    row = x * 2 + c
    me = row * 4 + y
    half = z // 4
    zy = rem(z, 4)
    owner = zy == y

    def each(lo, hi, f):
        def body(t, _):
            f(t)
            return 0
        lax.fori_loop(lo, hi, body, 0)

    cl = pltpu.make_async_copy(left_h, left, lsem.at[0])
    cr = pltpu.make_async_copy(right_h, right, lsem.at[1])
    cl.start()
    cr.start()

    barrier = pltpu.get_barrier_semaphore()

    def greet(dev):
        pl.semaphore_signal(barrier, inc=1, device_id=dev, device_id_type=MESH)

    def plane_dev(q):
        px, pc, py = plane_peer(q)
        return (z, px, pc, py)

    each(1, 32, lambda t: greet(plane_dev(rem(me + t, 32))))
    each(1, 8, lambda t: greet((rem(z + t, 8), x, c, zy)))
    for h in range(2):
        @pl.when(z != h * 4 + y)
        def _(h=h):
            for v in range(4):
                greet((h * 4 + y, x, c, v))

    pack[0:128, :] = dens[...]
    pack[128:176, :] = pos[...]
    pack[176:192, :] = area[...]
    t1[...] = jnp.zeros_like(t1)
    t2[...] = jnp.zeros_like(t2)
    t1[:, 0:64] = near[...]
    t2[0:1, 0:64] = ncnt[...]
    t2[1:2, 0:64] = far[1:2, :]
    t2[2:3, 0:64] = far[3:4, :]
    lane8 = lax.broadcasted_iota(i32, (8, 128), 1)
    igy[y] = jnp.where(lane8 < 64, t1[...], pltpu.roll(t2[...], 64, 1))

    def quarter(n):
        return pl.ds(pl.multiple_of(y * n, n), n)

    @pl.when(owner)
    def _():
        pb[half, quarter(48), :] = pack[quarter(48), :]
        pl.semaphore_wait(barrier, 42)

    @pl.when(jnp.logical_not(owner))
    def _():
        pl.semaphore_wait(barrier, 46)

    def remote(src, dst, ss, rs, dev):
        return pltpu.make_async_remote_copy(src_ref=src, dst_ref=dst, send_sem=ss, recv_sem=rs,
                                            device_id=dev, device_id_type=MESH)

    side = (z, x, c, rem(y + 1, 4))

    def copy_b(t):
        return remote(pack.at[quarter(48)], pb.at[half, quarter(48)], s_b, r_b.at[half], (rem(z + t, 8), x, c, zy))

    for t in (4, 3, 5, 2, 6, 1, 7):
        copy_b(t).start()

    @pl.when(jnp.logical_not(owner))
    def _():
        copy_b(0).start()

    def step_y(src, dst, k):
        for t in range(1, 4):
            yy = rem(y + t, 4)
            remote(src(yy), dst.at[y], s_y.at[k], r_y.at[k], (z, x, c, yy)).start()

    def wait_y(dst, k):
        w = dst.at[pl.ds(0, 3)]
        remote(w, w, s_y.at[k], r_y.at[k], side).wait_recv()

    def step_row(src, dst, k):
        def one(t):
            p = rem(row + 8 - t, 8)
            remote(src.at[:, p], dst.at[row], s_r.at[k], r_r.at[k], (z, p // 2, rem(p, 2), y)).start()
        each(1, 8, one)

    def wait_row(dst, k):
        w = dst.at[pl.ds(0, 7)]
        remote(w, w, s_r.at[k], r_r.at[k], side).wait_recv()

    step_y(lambda yy: igy.at[y], igy, 0)

    def copy_a(t, slot):
        p = rem(row + 8 - t, 8)
        return remote(pack, pa.at[slot], s_a, r_a.at[slot], (z, p // 2, rem(p, 2), y))

    def tables(load, dref, base):
        for k in range(8):
            v = load(16 * k).astype(f32)
            dref[base + 2 * k] = v[:8]
            dref[base + 2 * k + 1] = v[8:]

    def prep(load, par):
        feats(load, vl, True)
        for k in range(16):
            lf[par * 16 + k] = left_factor(rows8(vl, k))
        tables(load, da, par * 16)

    vl[...] = jnp.zeros_like(vl)
    prep(lambda o: pack[o:o + 16, :], 0)
    feats(lambda o: pack[o:o + 16, :], vl, False)
    own[...] = jnp.zeros_like(own)
    for s in range(4):
        k = 4 * y + s
        u = lax.rsqrt(jnp.dot(right_factor(rows8(vl, k)), lf[k], preferred_element_type=f32)).astype(bf16)
        own[pl.ds(pl.multiple_of(8 * k, 8), 8), :] = jnp.dot(da[k].astype(bf16), u, preferred_element_type=f32)

    kr = lax.broadcasted_iota(i32, (64, 256), 0) // 8
    kc = lax.broadcasted_iota(i32, (64, 256), 1) // 32
    mask = jnp.where(kr == kc, 1.0, 0.0)

    def far_owner(p, yy, h):
        return h * 32 + yy * 8 + p

    def far_cols(p):
        for v in range(2):
            es = [far_owner(p, yy, h) for yy in (2 * v, 2 * v + 1) for h in range(2)]
            ds = []
            for e in es:
                for k in range(2):
                    i = rem(fars[2 * k, e], 16)
                    ds.append(jnp.where(k < fcnts[0, e], da[i], 0.0))
            r = through(jnp.concatenate(ds, 0).astype(bf16), jnp.concatenate([left[e] for e in es], 0),
                        jnp.concatenate([right[e] for e in es], 0), mask).astype(bf16)
            fc[2 * v, p] = r[:32]
            fc[2 * v + 1, p] = r[32:]

    cl.wait()
    cr.wait()
    def far_cols2(u):
        far_cols(2 * u)
        far_cols(2 * u + 1)

    each(0, 2, far_cols2)

    wait_y(igy, 0)
    own_i = pltpu.make_async_copy(igy, igot.at[row], lsem.at[0])
    own_i.start()

    def send_i(t):
        p = rem(row + 8 - t, 8)
        remote(igy, igot.at[row], s_r.at[0], r_r.at[0], (z, p // 2, rem(p, 2), y)).start()

    each(1, 8, send_i)
    each(1, 8, lambda t: copy_a(t, row).start())
    each(2, 4, far_cols2)
    step_y(lambda yy: fc.at[yy], fcy, 1)
    own_c = pltpu.make_async_copy(fc.at[y], fcy.at[y], lsem.at[1])
    own_c.start()


    own_i.wait()
    wait_row(igot, 0)
    q0 = y * 8 + row
    lists = jnp.zeros((8, 128), i32)
    for s in range(32):
        lists = jnp.where(rem(lane8, 32) == s, pltpu.roll(igot[s // 4, s % 4], rem(s - q0 + 128, 128), 1), lists)
    cvm[...] = lists
    ci = pltpu.make_async_copy(cvm, csm, lsem.at[2])
    ci.start()
    for h in range(2):
        w4 = pb.at[h]
        w3 = pb.at[h, pl.ds(0, 144)]

        @pl.when(z != h * 4 + y)
        def _(w4=w4, h=h):
            remote(w4, w4, s_b, r_b.at[h], side).wait_recv()

        @pl.when(z == h * 4 + y)
        def _(w3=w3, h=h):
            remote(w3, w3, s_b, r_b.at[h], side).wait_recv()

    for h in range(2):
        feats(lambda o, h=h: pb[h, o:o + 16, :], vl, False)
        for k in range(16):
            rt[h * 16 + k] = right_factor(rows8(vl, k))
        tables(lambda o, h=h: pb[h, o:o + 16, :], db, h * 16)
    ci.wait()

    def far_col(s, h, k):
        return h * 16 + rem(csm[1 + k, 64 + h * 32 + s], 16)

    def fill_fd(p):
        for yy in range(4):
            s = p * 4 + yy
            fd[yy, p] = jnp.concatenate([db[far_col(s, h, k)] for h in range(2) for k in range(2)], 0).astype(bf16)

    each(0, 8, fill_fd)
    own_c.wait()
    own_d = pltpu.make_async_copy(fd.at[y], fdy.at[y], lsem.at[0])
    own_d.start()
    step_y(lambda yy: fd.at[yy], fdy, 2)
    own_d.wait()

    def slot_ids(b, n):
        s, h, k = 4 * b + n // 8, (n // 4) % 2, n % 4
        return (rem(csm[2 * k, h * 32 + s], 16), h * 16 + rem(csm[2 * k + 1, h * 32 + s], 16),
                k < csm[0, 64 + h * 32 + s])

    tiles = (ub0, ub1)

    def build(b, par, n):
        i, j, _ = slot_ids(b, n)
        d2 = jnp.dot(rt[j], lf[par * 16 + i], preferred_element_type=f32)
        tiles[n // 16][n % 16] = lax.rsqrt(d2).astype(bf16)

    def apply(b, par, n, rows=True, cols=True):
        i, j, _ = slot_ids(b, n)
        u = tiles[n // 16][n % 16]
        if rows:
            rbuf[8 * n:8 * n + 8, :] = jnp.dot(db[j].astype(bf16), u, preferred_element_type=f32)
        if cols:
            cbuf[8 * n:8 * n + 8, :] = lax.dot_general(
                da[par * 16 + i].astype(bf16), u, (((1,), (1,)), ((), ())), preferred_element_type=f32)

    def copy_oa(b, yy, slot):
        return remote(sa.at[b, pl.ds(pl.multiple_of(yy * 32, 32), 32)], ra.at[slot], s_oa, r_oa,
                      (z, b // 2, rem(b, 2), yy))

    def row_sums(b):
        ids = [slot_ids(b, n) for n in range(32)]
        return gathered(pick_matrix([jnp.where(v[2], v[0], -1) for v in ids], 128), rbuf[...])

    def col_sums(b):
        ids = [slot_ids(b, n) for n in range(32)]
        acc_b[...] += gathered(pick_matrix([jnp.where(v[2], v[1], -1) for v in ids], 256), cbuf[...])

    def send_oa(b):
        for v in range(4):
            copy_oa(b, rem(y + v, 4), me).start()

    acc_b[...] = jnp.zeros_like(acc_b)
    for n in range(16):
        build(row, 0, n)

    def group(t):
        b = rem(row + t, 8)
        nb = rem(row + t + 1, 8)
        par = rem(t, 2)
        copy_a(t + 1, nb).wait_recv()
        for n in range(16):
            apply(b, par, n)
            build(b, par, 16 + n)
        prep(lambda o: pa[nb, o:o + 16, :], 1 - par)
        for n in range(16):
            apply(b, par, 16 + n)
            build(nb, 1 - par, n)
        col_sums(b)
        sums = row_sums(b)

        @pl.when(t == 0)
        def _():
            own[...] += sums
            wait_y(fcy, 1)
            step_row(fcy, fcr, 1)

        @pl.when(t > 0)
        def _():
            sa[b] = sums.astype(bf16)
            send_oa(b)

        @pl.when(t == 2)
        def _():
            wait_y(fdy, 2)
            step_row(fdy, fdr, 2)

    each(0, 7, group)

    own_c2 = pltpu.make_async_copy(fcy.at[:, row], fcr.at[row], lsem.at[0])
    own_c2.start()
    own_d2 = pltpu.make_async_copy(fdy.at[:, row], fdr.at[row], lsem.at[1])
    own_d2.start()
    own_c2.wait()
    own_d2.wait()
    wait_row(fcr, 1)
    for g in range(4):
        ids = [far_col(g * 8 + n // 4, (n // 2) % 2, n % 2) for n in range(32)]
        v = jnp.concatenate([fcr[g * 2 + k // 4, k % 4] for k in range(8)], 0)
        acc_b[...] += jnp.dot(pick_matrix(ids, 256), v, preferred_element_type=f32)

    last = rem(row + 7, 8)
    for n in range(16):
        apply(last, 1, n, rows=False)
        build(last, 1, 16 + n)
    for n in range(16):
        apply(last, 1, 16 + n, rows=False)
    col_sums(last)
    for h in range(2):
        sb[h] = acc_b[128 * h:128 * h + 128, :].astype(bf16)

    def copy_ob(h, yy):
        return remote(sb.at[h, pl.ds(pl.multiple_of(yy * 32, 32), 32)], rb.at[z], s_ob, r_ob, (h * 4 + y, x, c, yy))

    for v in (1, 2, 3, 0):
        for h in range(2):
            if v == 0:
                @pl.when(z != h * 4 + y)
                def _(h=h):
                    copy_ob(h, y).start()
            else:
                copy_ob(h, rem(y + v, 4)).start()

    @pl.when(owner)
    def _():
        rb[z] = sb[half, quarter(32), :]

    for n in range(32):
        apply(last, 1, n, cols=False)
    sa[last] = row_sums(last).astype(bf16)
    send_oa(last)

    wait_row(fdr, 2)

    def far_rows(g):
        ids = []
        for b in range(4):
            p, yys = g * 2 + b // 2, (2 * (b % 2), 2 * (b % 2) + 1)
            es = [far_owner(p, yy, h) for yy in yys for h in range(2)]
            rbuf[64 * b:64 * b + 64, :] = through(
                jnp.concatenate([fdr[p, yy] for yy in yys], 0), jnp.concatenate([right[e] for e in es], 0),
                jnp.concatenate([left[e] for e in es], 0), mask)
            ids += [jnp.where(k < fcnts[0, e], rem(fars[2 * k, e], 16), -1) for e in es for k in range(2)]
        own[...] += gathered(pick_matrix(ids, 128), rbuf[...])

    each(0, 4, far_rows)

    sa[row] = own[...].astype(bf16)
    for v in range(1, 4):
        copy_oa(row, rem(y + v, 4), me).start()
    ra[me] = jnp.zeros((32, 256), bf16)
    part[...] = own[quarter(32), :]
    w = ra.at[pl.ds(0, 31)]
    remote(w, w, s_oa, r_oa, side).wait_recv()

    def add_a(t):
        part[...] += ((ra[4 * t].astype(f32) + ra[4 * t + 1].astype(f32))
                      + (ra[4 * t + 2].astype(f32) + ra[4 * t + 3].astype(f32)))

    each(0, 8, add_a)

    def both(f):
        @pl.when(owner)
        def _():
            f(rb.at[pl.ds(0, 7)])

        @pl.when(jnp.logical_not(owner))
        def _():
            f(rb)

    both(lambda v: remote(v, v, s_ob, r_ob, side).wait_recv())
    part[...] += (((rb[0].astype(f32) + rb[1].astype(f32)) + (rb[2].astype(f32) + rb[3].astype(f32)))
                  + ((rb[4].astype(f32) + rb[5].astype(f32)) + (rb[6].astype(f32) + rb[7].astype(f32))))

    for t in range(1, 4):
        remote(part, out.at[quarter(32)], s_o, r_o, (z, x, c, rem(y + t, 4))).start()
    out[quarter(32), :] = part[...]

    both(lambda v: remote(v, v, s_ob, r_ob, side).wait_send())
    remote(w, w, s_oa, r_oa, side).wait_send()
    w = pa.at[pl.ds(0, 7)]
    remote(w, w, s_a, r_a.at[0], side).wait_send()
    for k, (vy, vr) in enumerate(((igy, igot), (fcy, fcr), (fdy, fdr))):
        w = vy.at[pl.ds(0, 3)]
        remote(w, w, s_y.at[k], r_y.at[k], side).wait_send()
        w = vr.at[pl.ds(0, 7)]
        remote(w, w, s_r.at[k], r_r.at[k], side).wait_send()
    w = pa.at[0, pl.ds(0, 48)]
    n_b = 7

    def sent_b(t):
        remote(w, w, s_b, r_b.at[0], side).wait_send()

    each(0, n_b, sent_b)

    @pl.when(jnp.logical_not(owner))
    def _():
        sent_b(0)

    w = out.at[pl.ds(0, 96)]
    remote(w, w, s_o, r_o, side).wait_recv()
    remote(w, w, s_o, r_o, side).wait_send()


def per_device(density, positions, areas, near_pairs, near_counts, far_pairs, far_counts, far_right, far_left):
    near = near_pairs[0, 0].transpose(1, 2, 0).reshape(8, 64)
    far = far_pairs[0, 0].transpose(1, 2, 0).reshape(4, 64)
    ncnt = near_counts.reshape(1, 64)
    fcnt = far_counts.reshape(1, 64)
    left = far_left.reshape(64, 64, 256)
    right = far_right.reshape(64, 64, 256)
    vm = pl.BlockSpec(memory_space=pltpu.VMEM)
    sm = pl.BlockSpec(memory_space=pltpu.SMEM)
    hbm = pl.BlockSpec(memory_space=pl.ANY)
    V, D = pltpu.VMEM, pltpu.SemaphoreType.DMA
    out = pl.pallas_call(
        kernel,
        out_shape=jax.ShapeDtypeStruct((128, 256), f32),
        in_specs=[vm] * 6 + [sm] * 2 + [hbm] * 2,
        out_specs=vm,
        scratch_shapes=[
            V((64, 64, 256), bf16), V((64, 64, 256), bf16), V((192, 256), bf16), V((8, 192, 256), bf16),
            V((2, 192, 256), bf16), V((8, 128), i32), V((8, 128), i32), V((4, 8, 128), i32), V((8, 4, 8, 128), i32),
            V((8, 128), i32), pltpu.SMEM((8, 128), i32), V((2, 128, 128), f32), V((32, KF, 256), bf16),
            V((32, 256, KF), bf16), V((32, 8, 256), f32), V((32, 8, 256), f32),
            V((16, 256, 256), bf16), V((16, 256, 256), bf16), V((256, 256), f32), V((256, 256), f32), V((256, 256), f32), V((128, 256), f32),
            V((4, 8, 32, 256), bf16), V((4, 8, 32, 256), bf16), V((8, 4, 32, 256), bf16),
            V((4, 8, 32, 256), bf16), V((4, 8, 32, 256), bf16), V((8, 4, 32, 256), bf16),
            V((8, 128, 256), bf16), V((2, 128, 256), bf16), V((32, 32, 256), bf16), V((8, 32, 256), bf16),
            V((32, 256), f32),
            D((3,)), D, D((8,)), D, D((2,)), D((3,)), D((3,)), D((3,)), D((3,)), D, D, D, D, D, D,
        ],
        compiler_params=pltpu.CompilerParams(collective_id=1, has_side_effects=True,
                                             vmem_limit_bytes=56 * 1024 * 1024),
    )(near, ncnt, far, density.reshape(128, 256), positions.transpose(1, 0, 2).reshape(48, 256), areas,
      far, fcnt, left, right)
    return out.reshape(16, 8, 256)


def solution(mesh):
    grid = Mesh(mesh.devices.reshape(8, 4, 2, 4), ("z", "x", "c", "y"))
    d = ("z", "x", "c")
    return jax.shard_map(
        per_device,
        mesh=grid,
        in_specs=(
            P(d, None, None),
            P(d, None, None),
            P(d, None),
            P(d, "y", None, None, None),
            P(d, "y", None),
            P(d, "y", None, None, None),
            P(d, "y", None),
            P(d, "y", None, None, None, None),
            P(d, "y", None, None, None, None),
        ),
        out_specs=P(d, None, None),
        check_vma=False,
    )
```

```python
import jax
import jax.numpy as jnp
from jax import lax
from jax.experimental import pallas as pl
from jax.experimental.pallas import tpu as pltpu
from jax.sharding import Mesh, PartitionSpec as P

f32 = jnp.float32
bf16 = jnp.bfloat16
i32 = jnp.int32
MESH = pl.DeviceIdType.MESH
KF = 48


def rem(a, n):
    return lax.rem(a, jnp.int32(n))


def plane_peer(flat):
    return flat // 8, rem(flat // 4, 2), rem(flat, 4)


def split3(v):
    h = v.astype(bf16).astype(f32)
    m = (v - h).astype(bf16).astype(f32)
    return h, m, v - h - m


def feats(load, vref, left):
    xs = [load(128 + 16 * k).astype(f32) - 0.5 for k in range(3)]
    a = load(176).astype(f32)
    w = 256.0 / (a * a)
    n = (xs[0] * xs[0] + xs[1] * xs[1] + xs[2] * xs[2] + 0.005) * w
    rows = [n, w] if left else [w, n]
    rows += [v * ((-2.0 if left else 1.0) * w) for v in xs]
    for k, r in enumerate(rows):
        vref[0, pl.ds(k, 16, stride=8), :] = r[:, :128]
        vref[1, pl.ds(k, 16, stride=8), :] = r[:, 128:]


def rows8(vref, c):
    o = pl.ds(pl.multiple_of(8 * c, 8), 8)
    return jnp.concatenate([vref[0, o, :], vref[1, o, :]], 1)


def left_factor(v):
    h, m, l = split3(v)
    return jnp.concatenate([h, h, m, m, h, l], 0).astype(bf16)


def right_factor(v):
    h, m, l = split3(v)
    return jnp.concatenate([h, m, h, m, l, h], 0).T.astype(bf16)


def through(dens, first, second, mask):
    p = lax.dot_general(dens, first, (((1,), (1,)), ((), ())), preferred_element_type=f32)
    p = (p.astype(bf16).astype(f32) * mask).astype(bf16)
    return jnp.dot(p, second, preferred_element_type=f32)


def pick_matrix(ids, rows):
    lane = lax.broadcasted_iota(i32, (1, 256), 1)
    key = jnp.full((1, 256), -8, i32)
    for n, v in enumerate(ids):
        key = jnp.where(lane // 8 == n, v * 8, key)
    key = key + rem(lane, 8)
    return jnp.where(lax.broadcasted_iota(i32, (rows, 256), 0) == key, 1.0, 0.0).astype(bf16)


def gathered(sel, v):
    hi = v.astype(bf16)
    lo = (v - hi.astype(f32)).astype(bf16)
    return jnp.dot(sel, hi, preferred_element_type=f32) + jnp.dot(sel, lo, preferred_element_type=f32)


def kernel(near, ncnt, far, dens, pos, area, fars, fcnts, left_h, right_h, out,
           left, right, pack, pa, pb, t1, t2, igy, igot, cvm, csm, vl, lf, rt, da, db, ub0, ub1, rbuf, cbuf,
           acc_b, own, fc, fcy, fcr, fd, fdy, fdr, sa, sb, ra, rb, part,
           lsem, s_a, r_a, s_b, r_b, s_y, r_y, s_r, r_r, s_oa, r_oa, s_ob, r_ob, s_o, r_o):
    z, x, c, y = (lax.axis_index(n) for n in ("z", "x", "c", "y"))
    row = x * 2 + c
    me = row * 4 + y
    half = z // 4
    zy = rem(z, 4)
    owner = zy == y

    def each(lo, hi, f):
        def body(t, _):
            f(t)
            return 0
        lax.fori_loop(lo, hi, body, 0)

    cl = pltpu.make_async_copy(left_h, left, lsem.at[0])
    cr = pltpu.make_async_copy(right_h, right, lsem.at[1])
    cl.start()
    cr.start()

    barrier = pltpu.get_barrier_semaphore()

    def greet(dev):
        pl.semaphore_signal(barrier, inc=1, device_id=dev, device_id_type=MESH)

    def plane_dev(q):
        px, pc, py = plane_peer(q)
        return (z, px, pc, py)

    each(1, 32, lambda t: greet(plane_dev(rem(me + t, 32))))
    each(1, 8, lambda t: greet((rem(z + t, 8), x, c, zy)))
    for h in range(2):
        @pl.when(z != h * 4 + y)
        def _(h=h):
            for v in range(4):
                greet((h * 4 + y, x, c, v))

    pack[0:128, :] = dens[...]
    pack[128:176, :] = pos[...]
    pack[176:192, :] = area[...]
    t1[...] = jnp.zeros_like(t1)
    t2[...] = jnp.zeros_like(t2)
    t1[:, 0:64] = near[...]
    t2[0:1, 0:64] = ncnt[...]
    t2[1:2, 0:64] = far[1:2, :]
    t2[2:3, 0:64] = far[3:4, :]
    lane8 = lax.broadcasted_iota(i32, (8, 128), 1)
    igy[y] = jnp.where(lane8 < 64, t1[...], pltpu.roll(t2[...], 64, 1))

    def quarter(n):
        return pl.ds(pl.multiple_of(y * n, n), n)

    @pl.when(owner)
    def _():
        pb[half, quarter(48), :] = pack[quarter(48), :]
        pl.semaphore_wait(barrier, 42)

    @pl.when(jnp.logical_not(owner))
    def _():
        pl.semaphore_wait(barrier, 46)

    def remote(src, dst, ss, rs, dev):
        return pltpu.make_async_remote_copy(src_ref=src, dst_ref=dst, send_sem=ss, recv_sem=rs,
                                            device_id=dev, device_id_type=MESH)

    side = (z, x, c, rem(y + 1, 4))

    def copy_b(t):
        return remote(pack.at[quarter(48)], pb.at[half, quarter(48)], s_b, r_b.at[half], (rem(z + t, 8), x, c, zy))

    for t in (4, 3, 5, 2, 6, 1, 7):
        copy_b(t).start()

    @pl.when(jnp.logical_not(owner))
    def _():
        copy_b(0).start()

    def step_y(src, dst, k):
        for t in range(1, 4):
            yy = rem(y + t, 4)
            remote(src(yy), dst.at[y], s_y.at[k], r_y.at[k], (z, x, c, yy)).start()

    def wait_y(dst, k):
        w = dst.at[pl.ds(0, 3)]
        remote(w, w, s_y.at[k], r_y.at[k], side).wait_recv()

    def step_row(src, dst, k):
        def one(t):
            p = rem(row + 8 - t, 8)
            remote(src.at[:, p], dst.at[row], s_r.at[k], r_r.at[k], (z, p // 2, rem(p, 2), y)).start()
        each(1, 8, one)

    def wait_row(dst, k):
        w = dst.at[pl.ds(0, 7)]
        remote(w, w, s_r.at[k], r_r.at[k], side).wait_recv()

    step_y(lambda yy: igy.at[y], igy, 0)

    def copy_a(t, slot):
        p = rem(row + 8 - t, 8)
        return remote(pack, pa.at[slot], s_a, r_a.at[slot], (z, p // 2, rem(p, 2), y))

    def tables(load, dref, base):
        for k in range(8):
            v = load(16 * k).astype(f32)
            dref[base + 2 * k] = v[:8]
            dref[base + 2 * k + 1] = v[8:]

    def prep(load, par):
        feats(load, vl, True)
        for k in range(16):
            lf[par * 16 + k] = left_factor(rows8(vl, k))
        tables(load, da, par * 16)

    vl[...] = jnp.zeros_like(vl)
    prep(lambda o: pack[o:o + 16, :], 0)
    feats(lambda o: pack[o:o + 16, :], vl, False)
    own[...] = jnp.zeros_like(own)
    for s in range(4):
        k = 4 * y + s
        u = lax.rsqrt(jnp.dot(right_factor(rows8(vl, k)), lf[k], preferred_element_type=f32)).astype(bf16)
        own[pl.ds(pl.multiple_of(8 * k, 8), 8), :] = jnp.dot(da[k].astype(bf16), u, preferred_element_type=f32)

    kr = lax.broadcasted_iota(i32, (64, 256), 0) // 8
    kc = lax.broadcasted_iota(i32, (64, 256), 1) // 32
    mask = jnp.where(kr == kc, 1.0, 0.0)

    def far_owner(p, yy, h):
        return h * 32 + yy * 8 + p

    def far_cols(p):
        for v in range(2):
            es = [far_owner(p, yy, h) for yy in (2 * v, 2 * v + 1) for h in range(2)]
            ds = []
            for e in es:
                for k in range(2):
                    i = rem(fars[2 * k, e], 16)
                    ds.append(jnp.where(k < fcnts[0, e], da[i], 0.0))
            r = through(jnp.concatenate(ds, 0).astype(bf16), jnp.concatenate([left[e] for e in es], 0),
                        jnp.concatenate([right[e] for e in es], 0), mask).astype(bf16)
            fc[2 * v, p] = r[:32]
            fc[2 * v + 1, p] = r[32:]

    cl.wait()
    cr.wait()
    def far_cols2(u):
        far_cols(2 * u)
        far_cols(2 * u + 1)

    each(0, 2, far_cols2)

    wait_y(igy, 0)
    own_i = pltpu.make_async_copy(igy, igot.at[row], lsem.at[0])
    own_i.start()

    def send_i(t):
        p = rem(row + 8 - t, 8)
        remote(igy, igot.at[row], s_r.at[0], r_r.at[0], (z, p // 2, rem(p, 2), y)).start()

    each(1, 8, send_i)
    each(1, 8, lambda t: copy_a(t, row).start())
    each(2, 4, far_cols2)
    step_y(lambda yy: fc.at[yy], fcy, 1)
    own_c = pltpu.make_async_copy(fc.at[y], fcy.at[y], lsem.at[1])
    own_c.start()


    own_i.wait()
    wait_row(igot, 0)
    q0 = y * 8 + row
    lists = jnp.zeros((8, 128), i32)
    for s in range(32):
        lists = jnp.where(rem(lane8, 32) == s, pltpu.roll(igot[s // 4, s % 4], rem(s - q0 + 128, 128), 1), lists)
    cvm[...] = rem(lists, 16)
    ci = pltpu.make_async_copy(cvm, csm, lsem.at[2])
    ci.start()
    for h in range(2):
        w4 = pb.at[h]
        w3 = pb.at[h, pl.ds(0, 144)]

        @pl.when(z != h * 4 + y)
        def _(w4=w4, h=h):
            remote(w4, w4, s_b, r_b.at[h], side).wait_recv()

        @pl.when(z == h * 4 + y)
        def _(w3=w3, h=h):
            remote(w3, w3, s_b, r_b.at[h], side).wait_recv()

    for h in range(2):
        feats(lambda o, h=h: pb[h, o:o + 16, :], vl, False)
        for k in range(16):
            rt[h * 16 + k] = right_factor(rows8(vl, k))
        tables(lambda o, h=h: pb[h, o:o + 16, :], db, h * 16)
    ci.wait()

    def far_col(s, h, k):
        return h * 16 + csm[1 + k, 64 + h * 32 + s]

    def fill_fd(p):
        for yy in range(4):
            s = p * 4 + yy
            fd[yy, p] = jnp.concatenate([db[far_col(s, h, k)] for h in range(2) for k in range(2)], 0).astype(bf16)

    each(0, 8, fill_fd)
    own_c.wait()
    own_d = pltpu.make_async_copy(fd.at[y], fdy.at[y], lsem.at[0])
    own_d.start()
    step_y(lambda yy: fd.at[yy], fdy, 2)
    own_c2 = pltpu.make_async_copy(fcy.at[:, row], fcr.at[row], lsem.at[3])
    own_d2 = pltpu.make_async_copy(fdy.at[:, row], fdr.at[row], lsem.at[4])

    def slot_ids(b, n):
        s, h, k = 4 * b + n // 8, (n // 4) % 2, n % 4
        return (csm[2 * k, h * 32 + s], h * 16 + csm[2 * k + 1, h * 32 + s],
                k < csm[0, 64 + h * 32 + s])

    tiles = (ub0, ub1)

    def build(b, par, n):
        i, j, _ = slot_ids(b, n)
        d2 = jnp.dot(rt[j], lf[par * 16 + i], preferred_element_type=f32)
        tiles[n // 16][n % 16] = lax.rsqrt(d2).astype(bf16)

    def apply(b, par, n, rows=True, cols=True):
        i, j, _ = slot_ids(b, n)
        u = tiles[n // 16][n % 16]
        if rows:
            rbuf[8 * n:8 * n + 8, :] = jnp.dot(db[j].astype(bf16), u, preferred_element_type=f32)
        if cols:
            cbuf[8 * n:8 * n + 8, :] = lax.dot_general(
                da[par * 16 + i].astype(bf16), u, (((1,), (1,)), ((), ())), preferred_element_type=f32)

    def copy_oa(b, yy, slot):
        return remote(sa.at[b, pl.ds(pl.multiple_of(yy * 32, 32), 32)], ra.at[slot], s_oa, r_oa,
                      (z, b // 2, rem(b, 2), yy))

    def row_sums(b):
        ids = [slot_ids(b, n) for n in range(32)]
        return gathered(pick_matrix([jnp.where(v[2], v[0], -1) for v in ids], 128), rbuf[...])

    def col_sums(b):
        ids = [slot_ids(b, n) for n in range(32)]
        acc_b[...] += gathered(pick_matrix([jnp.where(v[2], v[1], -1) for v in ids], 256), cbuf[...])

    def send_oa(b):
        for v in range(4):
            copy_oa(b, rem(y + v, 4), me).start()

    acc_b[...] = jnp.zeros_like(acc_b)
    for n in range(16):
        build(row, 0, n)

    def group(t):
        b = rem(row + t, 8)
        nb = rem(row + t + 1, 8)
        par = rem(t, 2)
        copy_a(t + 1, nb).wait_recv()
        for n in range(16):
            apply(b, par, n)
            build(b, par, 16 + n)
        prep(lambda o: pa[nb, o:o + 16, :], 1 - par)
        for n in range(16):
            apply(b, par, 16 + n)
            build(nb, 1 - par, n)
        col_sums(b)
        sums = row_sums(b)

        @pl.when(t == 0)
        def _():
            own[...] += sums
            wait_y(fcy, 1)
            step_row(fcy, fcr, 1)
            own_c2.start()

        @pl.when(t > 0)
        def _():
            sa[b] = sums.astype(bf16)
            send_oa(b)

        @pl.when(t == 2)
        def _():
            wait_y(fdy, 2)
            own_d.wait()
            step_row(fdy, fdr, 2)
            own_d2.start()

    each(0, 7, group)

    own_c2.wait()
    wait_row(fcr, 1)
    for g in range(4):
        ids = [far_col(g * 8 + n // 4, (n // 2) % 2, n % 2) for n in range(32)]
        v = jnp.concatenate([fcr[g * 2 + k // 4, k % 4] for k in range(8)], 0)
        acc_b[...] += jnp.dot(pick_matrix(ids, 256), v, preferred_element_type=f32)

    last = rem(row + 7, 8)
    for n in range(16):
        apply(last, 1, n, rows=False)
        build(last, 1, 16 + n)
    for n in range(16):
        apply(last, 1, 16 + n, rows=False)
    col_sums(last)
    for h in range(2):
        sb[h] = acc_b[128 * h:128 * h + 128, :].astype(bf16)

    def copy_ob(h, yy):
        return remote(sb.at[h, pl.ds(pl.multiple_of(yy * 32, 32), 32)], rb.at[z], s_ob, r_ob, (h * 4 + y, x, c, yy))

    for v in (1, 2, 3, 0):
        for h in range(2):
            if v == 0:
                @pl.when(z != h * 4 + y)
                def _(h=h):
                    copy_ob(h, y).start()
            else:
                copy_ob(h, rem(y + v, 4)).start()

    @pl.when(owner)
    def _():
        rb[z] = sb[half, quarter(32), :]

    for n in range(32):
        apply(last, 1, n, cols=False)
    sa[last] = row_sums(last).astype(bf16)
    send_oa(last)

    own_d2.wait()
    wait_row(fdr, 2)

    def far_rows(g):
        ids = []
        for b in range(4):
            p, yys = g * 2 + b // 2, (2 * (b % 2), 2 * (b % 2) + 1)
            es = [far_owner(p, yy, h) for yy in yys for h in range(2)]
            rbuf[64 * b:64 * b + 64, :] = through(
                jnp.concatenate([fdr[p, yy] for yy in yys], 0), jnp.concatenate([right[e] for e in es], 0),
                jnp.concatenate([left[e] for e in es], 0), mask)
            ids += [jnp.where(k < fcnts[0, e], rem(fars[2 * k, e], 16), -1) for e in es for k in range(2)]
        own[...] += gathered(pick_matrix(ids, 128), rbuf[...])

    each(0, 4, far_rows)

    sa[row] = own[...].astype(bf16)
    for v in range(1, 4):
        copy_oa(row, rem(y + v, 4), me).start()
    ra[me] = jnp.zeros((32, 256), bf16)
    part[...] = own[quarter(32), :]
    w = ra.at[pl.ds(0, 31)]
    remote(w, w, s_oa, r_oa, side).wait_recv()

    def add_a(t):
        part[...] += ((ra[4 * t].astype(f32) + ra[4 * t + 1].astype(f32))
                      + (ra[4 * t + 2].astype(f32) + ra[4 * t + 3].astype(f32)))

    each(0, 8, add_a)

    def both(f):
        @pl.when(owner)
        def _():
            f(rb.at[pl.ds(0, 7)])

        @pl.when(jnp.logical_not(owner))
        def _():
            f(rb)

    both(lambda v: remote(v, v, s_ob, r_ob, side).wait_recv())
    part[...] += (((rb[0].astype(f32) + rb[1].astype(f32)) + (rb[2].astype(f32) + rb[3].astype(f32)))
                  + ((rb[4].astype(f32) + rb[5].astype(f32)) + (rb[6].astype(f32) + rb[7].astype(f32))))

    for t in range(1, 4):
        remote(part, out.at[quarter(32)], s_o, r_o, (z, x, c, rem(y + t, 4))).start()
    out[quarter(32), :] = part[...]

    both(lambda v: remote(v, v, s_ob, r_ob, side).wait_send())
    remote(w, w, s_oa, r_oa, side).wait_send()
    w = pa.at[pl.ds(0, 7)]
    remote(w, w, s_a, r_a.at[0], side).wait_send()
    for k, (vy, vr) in enumerate(((igy, igot), (fcy, fcr), (fdy, fdr))):
        w = vy.at[pl.ds(0, 3)]
        remote(w, w, s_y.at[k], r_y.at[k], side).wait_send()
        w = vr.at[pl.ds(0, 7)]
        remote(w, w, s_r.at[k], r_r.at[k], side).wait_send()
    w = pa.at[0, pl.ds(0, 48)]
    n_b = 7

    def sent_b(t):
        remote(w, w, s_b, r_b.at[0], side).wait_send()

    each(0, n_b, sent_b)

    @pl.when(jnp.logical_not(owner))
    def _():
        sent_b(0)

    w = out.at[pl.ds(0, 96)]
    remote(w, w, s_o, r_o, side).wait_recv()
    remote(w, w, s_o, r_o, side).wait_send()


def per_device(density, positions, areas, near_pairs, near_counts, far_pairs, far_counts, far_right, far_left):
    near = near_pairs[0, 0].transpose(1, 2, 0).reshape(8, 64)
    far = far_pairs[0, 0].transpose(1, 2, 0).reshape(4, 64)
    ncnt = near_counts.reshape(1, 64)
    fcnt = far_counts.reshape(1, 64)
    left = far_left.reshape(64, 64, 256)
    right = far_right.reshape(64, 64, 256)
    vm = pl.BlockSpec(memory_space=pltpu.VMEM)
    sm = pl.BlockSpec(memory_space=pltpu.SMEM)
    hbm = pl.BlockSpec(memory_space=pl.ANY)
    V, D = pltpu.VMEM, pltpu.SemaphoreType.DMA
    out = pl.pallas_call(
        kernel,
        out_shape=jax.ShapeDtypeStruct((128, 256), f32),
        in_specs=[vm] * 6 + [sm] * 2 + [hbm] * 2,
        out_specs=vm,
        scratch_shapes=[
            V((64, 64, 256), bf16), V((64, 64, 256), bf16), V((192, 256), bf16), V((8, 192, 256), bf16),
            V((2, 192, 256), bf16), V((8, 128), i32), V((8, 128), i32), V((4, 8, 128), i32), V((8, 4, 8, 128), i32),
            V((8, 128), i32), pltpu.SMEM((8, 128), i32), V((2, 128, 128), f32), V((32, KF, 256), bf16),
            V((32, 256, KF), bf16), V((32, 8, 256), f32), V((32, 8, 256), f32),
            V((16, 256, 256), bf16), V((16, 256, 256), bf16), V((256, 256), f32), V((256, 256), f32), V((256, 256), f32), V((128, 256), f32),
            V((4, 8, 32, 256), bf16), V((4, 8, 32, 256), bf16), V((8, 4, 32, 256), bf16),
            V((4, 8, 32, 256), bf16), V((4, 8, 32, 256), bf16), V((8, 4, 32, 256), bf16),
            V((8, 128, 256), bf16), V((2, 128, 256), bf16), V((32, 32, 256), bf16), V((8, 32, 256), bf16),
            V((32, 256), f32),
            D((5,)), D, D((8,)), D, D((2,)), D((3,)), D((3,)), D((3,)), D((3,)), D, D, D, D, D, D,
        ],
        compiler_params=pltpu.CompilerParams(collective_id=1, has_side_effects=True,
                                             vmem_limit_bytes=56 * 1024 * 1024),
    )(near, ncnt, far, density.reshape(128, 256), positions.transpose(1, 0, 2).reshape(48, 256), areas,
      far, fcnt, left, right)
    return out.reshape(16, 8, 256)


def solution(mesh):
    grid = Mesh(mesh.devices.reshape(8, 4, 2, 4), ("z", "x", "c", "y"))
    d = ("z", "x", "c")
    return jax.shard_map(
        per_device,
        mesh=grid,
        in_specs=(
            P(d, None, None),
            P(d, None, None),
            P(d, None),
            P(d, "y", None, None, None),
            P(d, "y", None),
            P(d, "y", None, None, None),
            P(d, "y", None),
            P(d, "y", None, None, None, None),
            P(d, "y", None, None, None, None),
        ),
        out_specs=P(d, None, None),
        check_vma=False,
    )
```

```python
import jax
import jax.numpy as jnp
from jax import lax
from jax.experimental import pallas as pl
from jax.experimental.pallas import tpu as pltpu
from jax.sharding import Mesh, PartitionSpec as P

f32 = jnp.float32
bf16 = jnp.bfloat16
i32 = jnp.int32
MESH = pl.DeviceIdType.MESH
KF = 48


def rem(a, n):
    return lax.rem(a, jnp.int32(n))


def plane_peer(flat):
    return flat // 8, rem(flat // 4, 2), rem(flat, 4)


def split3(v):
    h = v.astype(bf16).astype(f32)
    m = (v - h).astype(bf16).astype(f32)
    return h, m, v - h - m


def feats(load, vref, left):
    xs = [load(128 + 16 * k).astype(f32) - 0.5 for k in range(3)]
    a = load(176).astype(f32)
    w = 256.0 / (a * a)
    n = (xs[0] * xs[0] + xs[1] * xs[1] + xs[2] * xs[2] + 0.005) * w
    rows = [n, w] if left else [w, n]
    rows += [v * ((-2.0 if left else 1.0) * w) for v in xs]
    for k, r in enumerate(rows):
        vref[0, pl.ds(k, 16, stride=8), :] = r[:, :128]
        vref[1, pl.ds(k, 16, stride=8), :] = r[:, 128:]


def rows8(vref, c):
    o = pl.ds(pl.multiple_of(8 * c, 8), 8)
    return jnp.concatenate([vref[0, o, :], vref[1, o, :]], 1)


def left_factor(v):
    h, m, l = split3(v)
    return jnp.concatenate([h, h, m, m, h, l], 0).astype(bf16)


def right_factor(v):
    h, m, l = split3(v)
    return jnp.concatenate([h, m, h, m, l, h], 0).T.astype(bf16)


def through(dens, first, second, mask):
    p = lax.dot_general(dens, first, (((1,), (1,)), ((), ())), preferred_element_type=f32)
    p = (p.astype(bf16).astype(f32) * mask).astype(bf16)
    return jnp.dot(p, second, preferred_element_type=f32)


def pick_matrix(ids, rows):
    lane = lax.broadcasted_iota(i32, (1, 256), 1)
    key = jnp.full((1, 256), -8, i32)
    for n, v in enumerate(ids):
        key = jnp.where(lane // 8 == n, v * 8, key)
    key = key + rem(lane, 8)
    return jnp.where(lax.broadcasted_iota(i32, (rows, 256), 0) == key, 1.0, 0.0).astype(bf16)


def gathered(sel, v):
    hi = v.astype(bf16)
    lo = (v - hi.astype(f32)).astype(bf16)
    return jnp.dot(sel, hi, preferred_element_type=f32) + jnp.dot(sel, lo, preferred_element_type=f32)


def kernel(near, ncnt, far, dens, pos, area, fars, fcnts, left_h, right_h, out,
           left, right, pack, pa, pb, t1, t2, igy, igot, cvm, csm, vl, lf, rt, da, db, ub0, ub1, rbuf, cbuf,
           acc_b, own, fc, fcy, fcr, fd, fdy, fdr, sa, sb, ra, rb, part,
           lsem, s_a, r_a, s_b, r_b, s_y, r_y, s_r, r_r, s_oa, r_oa, s_ob, r_ob, s_o, r_o):
    z, x, c, y = (lax.axis_index(n) for n in ("z", "x", "c", "y"))
    row = x * 2 + c
    me = row * 4 + y
    half = z // 4
    zy = rem(z, 4)
    owner = zy == y

    def each(lo, hi, f):
        def body(t, _):
            f(t)
            return 0
        lax.fori_loop(lo, hi, body, 0)

    cl = pltpu.make_async_copy(left_h, left, lsem.at[0])
    cr = pltpu.make_async_copy(right_h, right, lsem.at[1])
    cl.start()
    cr.start()

    barrier = pltpu.get_barrier_semaphore()

    def greet(dev):
        pl.semaphore_signal(barrier, inc=1, device_id=dev, device_id_type=MESH)

    def plane_dev(q):
        px, pc, py = plane_peer(q)
        return (z, px, pc, py)

    each(1, 32, lambda t: greet(plane_dev(rem(me + t, 32))))
    each(1, 8, lambda t: greet((rem(z + t, 8), x, c, zy)))
    for h in range(2):
        @pl.when(z != h * 4 + y)
        def _(h=h):
            for v in range(4):
                greet((h * 4 + y, x, c, v))

    pack[0:128, :] = dens[...]
    pack[128:176, :] = pos[...]
    pack[176:192, :] = area[...]
    t1[...] = jnp.zeros_like(t1)
    t2[...] = jnp.zeros_like(t2)
    t1[:, 0:64] = near[...]
    t2[0:1, 0:64] = ncnt[...]
    t2[1:2, 0:64] = far[1:2, :]
    t2[2:3, 0:64] = far[3:4, :]
    lane8 = lax.broadcasted_iota(i32, (8, 128), 1)
    igy[y] = jnp.where(lane8 < 64, t1[...], pltpu.roll(t2[...], 64, 1))

    def quarter(n):
        return pl.ds(pl.multiple_of(y * n, n), n)

    @pl.when(owner)
    def _():
        pb[half, quarter(48), :] = pack[quarter(48), :]
        pl.semaphore_wait(barrier, 42)

    @pl.when(jnp.logical_not(owner))
    def _():
        pl.semaphore_wait(barrier, 46)

    def remote(src, dst, ss, rs, dev):
        return pltpu.make_async_remote_copy(src_ref=src, dst_ref=dst, send_sem=ss, recv_sem=rs,
                                            device_id=dev, device_id_type=MESH)

    side = (z, x, c, rem(y + 1, 4))

    def copy_b(t):
        return remote(pack.at[quarter(48)], pb.at[half, quarter(48)], s_b, r_b.at[half], (rem(z + t, 8), x, c, zy))

    for t in (4, 3, 5, 2, 6, 1, 7):
        copy_b(t).start()

    @pl.when(jnp.logical_not(owner))
    def _():
        copy_b(0).start()

    def step_y(src, dst, k):
        for t in range(1, 4):
            yy = rem(y + t, 4)
            remote(src(yy), dst.at[y], s_y.at[k], r_y.at[k], (z, x, c, yy)).start()

    def wait_y(dst, k):
        w = dst.at[pl.ds(0, 3)]
        remote(w, w, s_y.at[k], r_y.at[k], side).wait_recv()

    def step_row(src, dst, k):
        def one(t):
            p = rem(row + 8 - t, 8)
            remote(src.at[:, p], dst.at[row], s_r.at[k], r_r.at[k], (z, p // 2, rem(p, 2), y)).start()
        each(1, 8, one)

    def wait_row(dst, k):
        w = dst.at[pl.ds(0, 7)]
        remote(w, w, s_r.at[k], r_r.at[k], side).wait_recv()

    step_y(lambda yy: igy.at[y], igy, 0)

    def copy_a(t, slot):
        p = rem(row + 8 - t, 8)
        return remote(pack, pa.at[slot], s_a, r_a.at[slot], (z, p // 2, rem(p, 2), y))

    def tables(load, dref, base):
        for k in range(8):
            v = load(16 * k).astype(f32)
            dref[base + 2 * k] = v[:8]
            dref[base + 2 * k + 1] = v[8:]

    def prep(load, par):
        feats(load, vl, True)
        for k in range(16):
            lf[par * 16 + k] = left_factor(rows8(vl, k))
        tables(load, da, par * 16)

    vl[...] = jnp.zeros_like(vl)
    prep(lambda o: pack[o:o + 16, :], 0)
    feats(lambda o: pack[o:o + 16, :], vl, False)
    own[...] = jnp.zeros_like(own)
    for s in range(4):
        k = 4 * y + s
        u = lax.rsqrt(jnp.dot(right_factor(rows8(vl, k)), lf[k], preferred_element_type=f32)).astype(bf16)
        own[pl.ds(pl.multiple_of(8 * k, 8), 8), :] = jnp.dot(da[k].astype(bf16), u, preferred_element_type=f32)

    kr = lax.broadcasted_iota(i32, (64, 256), 0) // 8
    kc = lax.broadcasted_iota(i32, (64, 256), 1) // 32
    mask = jnp.where(kr == kc, 1.0, 0.0)

    def far_owner(p, yy, h):
        return h * 32 + yy * 8 + p

    def far_cols(p):
        for v in range(2):
            es = [far_owner(p, yy, h) for yy in (2 * v, 2 * v + 1) for h in range(2)]
            ds = []
            for e in es:
                for k in range(2):
                    i = rem(fars[2 * k, e], 16)
                    ds.append(jnp.where(k < fcnts[0, e], da[i], 0.0))
            r = through(jnp.concatenate(ds, 0).astype(bf16), jnp.concatenate([left[e] for e in es], 0),
                        jnp.concatenate([right[e] for e in es], 0), mask).astype(bf16)
            fc[2 * v, p] = r[:32]
            fc[2 * v + 1, p] = r[32:]

    cl.wait()
    cr.wait()
    def far_cols2(u):
        far_cols(2 * u)
        far_cols(2 * u + 1)

    each(0, 2, far_cols2)

    wait_y(igy, 0)
    own_i = pltpu.make_async_copy(igy, igot.at[row], lsem.at[0])
    own_i.start()

    def send_i(t):
        p = rem(row + 8 - t, 8)
        remote(igy, igot.at[row], s_r.at[0], r_r.at[0], (z, p // 2, rem(p, 2), y)).start()

    each(1, 8, send_i)
    each(1, 8, lambda t: copy_a(t, row).start())
    each(2, 4, far_cols2)
    step_y(lambda yy: fc.at[yy], fcy, 1)
    own_c = pltpu.make_async_copy(fc.at[y], fcy.at[y], lsem.at[1])
    own_c.start()


    own_i.wait()
    wait_row(igot, 0)
    q0 = y * 8 + row
    lists = jnp.zeros((8, 128), i32)
    for s in range(32):
        lists = jnp.where(rem(lane8, 32) == s, pltpu.roll(igot[s // 4, s % 4], rem(s - q0 + 128, 128), 1), lists)
    cvm[...] = rem(lists, 16)
    ci = pltpu.make_async_copy(cvm, csm, lsem.at[2])
    ci.start()
    for h in range(2):
        w4 = pb.at[h]
        w3 = pb.at[h, pl.ds(0, 144)]

        @pl.when(z != h * 4 + y)
        def _(w4=w4, h=h):
            remote(w4, w4, s_b, r_b.at[h], side).wait_recv()

        @pl.when(z == h * 4 + y)
        def _(w3=w3, h=h):
            remote(w3, w3, s_b, r_b.at[h], side).wait_recv()

    for h in range(2):
        feats(lambda o, h=h: pb[h, o:o + 16, :], vl, False)
        for k in range(16):
            rt[h * 16 + k] = right_factor(rows8(vl, k))
        tables(lambda o, h=h: pb[h, o:o + 16, :], db, h * 16)
    ci.wait()

    def far_col(s, h, k):
        return h * 16 + csm[1 + k, 64 + h * 32 + s]

    def fill_fd(p):
        for yy in range(4):
            s = p * 4 + yy
            fd[yy, p] = jnp.concatenate([db[far_col(s, h, k)] for h in range(2) for k in range(2)], 0).astype(bf16)

    each(0, 8, fill_fd)
    own_c.wait()
    own_d = pltpu.make_async_copy(fd.at[y], fdy.at[y], lsem.at[0])
    own_d.start()
    step_y(lambda yy: fd.at[yy], fdy, 2)
    own_c2 = pltpu.make_async_copy(fcy.at[:, row], fcr.at[row], lsem.at[3])
    own_d2 = pltpu.make_async_copy(fdy.at[:, row], fdr.at[row], lsem.at[4])

    def slot_ids(b, n):
        s, h, k = 4 * b + n // 8, (n // 4) % 2, n % 4
        return (csm[2 * k, h * 32 + s], h * 16 + csm[2 * k + 1, h * 32 + s],
                k < csm[0, 64 + h * 32 + s])

    tiles = (ub0, ub1)

    def build(b, par, n):
        i, j, _ = slot_ids(b, n)
        d2 = jnp.dot(rt[j], lf[par * 16 + i], preferred_element_type=f32)
        tiles[n // 16][n % 16] = lax.rsqrt(d2).astype(bf16)

    def apply(b, par, n, rows=True, cols=True):
        i, j, _ = slot_ids(b, n)
        u = tiles[n // 16][n % 16]
        if rows:
            rbuf[8 * n:8 * n + 8, :] = jnp.dot(db[j].astype(bf16), u, preferred_element_type=f32)
        if cols:
            cbuf[8 * n:8 * n + 8, :] = lax.dot_general(
                da[par * 16 + i].astype(bf16), u, (((1,), (1,)), ((), ())), preferred_element_type=f32)

    def copy_oa(b, yy, slot):
        return remote(sa.at[b, pl.ds(pl.multiple_of(yy * 32, 32), 32)], ra.at[slot], s_oa, r_oa,
                      (z, b // 2, rem(b, 2), yy))

    def row_sums(b):
        ids = [slot_ids(b, n) for n in range(32)]
        return gathered(pick_matrix([jnp.where(v[2], v[0], -1) for v in ids], 128), rbuf[...])

    def col_sums(b):
        ids = [slot_ids(b, n) for n in range(32)]
        acc_b[...] += gathered(pick_matrix([jnp.where(v[2], v[1], -1) for v in ids], 256), cbuf[...])

    def send_oa(b):
        for v in range(4):
            copy_oa(b, rem(y + v, 4), me).start()

    acc_b[...] = jnp.zeros_like(acc_b)
    for n in range(16):
        build(row, 0, n)

    def group(t):
        b = rem(row + t, 8)
        nb = rem(row + t + 1, 8)
        par = rem(t, 2)
        for n in range(16):
            apply(b, par, n)
            build(b, par, 16 + n)
        copy_a(t + 1, nb).wait_recv()
        prep(lambda o: pa[nb, o:o + 16, :], 1 - par)
        for n in range(16):
            apply(b, par, 16 + n)
            build(nb, 1 - par, n)
        col_sums(b)
        sums = row_sums(b)

        @pl.when(t == 0)
        def _():
            own[...] += sums
            wait_y(fcy, 1)
            step_row(fcy, fcr, 1)
            own_c2.start()

        @pl.when(t > 0)
        def _():
            sa[b] = sums.astype(bf16)
            send_oa(b)

        @pl.when(t == 2)
        def _():
            wait_y(fdy, 2)
            own_d.wait()
            step_row(fdy, fdr, 2)
            own_d2.start()

    each(0, 7, group)

    own_c2.wait()
    wait_row(fcr, 1)
    for g in range(4):
        ids = [far_col(g * 8 + n // 4, (n // 2) % 2, n % 2) for n in range(32)]
        v = jnp.concatenate([fcr[g * 2 + k // 4, k % 4] for k in range(8)], 0)
        acc_b[...] += jnp.dot(pick_matrix(ids, 256), v, preferred_element_type=f32)

    last = rem(row + 7, 8)
    for n in range(16):
        apply(last, 1, n, rows=False)
        build(last, 1, 16 + n)
    for n in range(16):
        apply(last, 1, 16 + n, rows=False)
    col_sums(last)
    for h in range(2):
        sb[h] = acc_b[128 * h:128 * h + 128, :].astype(bf16)

    def copy_ob(h, yy):
        return remote(sb.at[h, pl.ds(pl.multiple_of(yy * 32, 32), 32)], rb.at[z], s_ob, r_ob, (h * 4 + y, x, c, yy))

    for v in (1, 2, 3, 0):
        for h in range(2):
            if v == 0:
                @pl.when(z != h * 4 + y)
                def _(h=h):
                    copy_ob(h, y).start()
            else:
                copy_ob(h, rem(y + v, 4)).start()

    @pl.when(owner)
    def _():
        rb[z] = sb[half, quarter(32), :]

    for n in range(32):
        apply(last, 1, n, cols=False)
    sa[last] = row_sums(last).astype(bf16)
    send_oa(last)

    own_d2.wait()
    wait_row(fdr, 2)

    def far_rows(g):
        ids = []
        for b in range(4):
            p, yys = g * 2 + b // 2, (2 * (b % 2), 2 * (b % 2) + 1)
            es = [far_owner(p, yy, h) for yy in yys for h in range(2)]
            rbuf[64 * b:64 * b + 64, :] = through(
                jnp.concatenate([fdr[p, yy] for yy in yys], 0), jnp.concatenate([right[e] for e in es], 0),
                jnp.concatenate([left[e] for e in es], 0), mask)
            ids += [jnp.where(k < fcnts[0, e], rem(fars[2 * k, e], 16), -1) for e in es for k in range(2)]
        own[...] += gathered(pick_matrix(ids, 128), rbuf[...])

    each(0, 4, far_rows)

    sa[row] = own[...].astype(bf16)
    for v in range(1, 4):
        copy_oa(row, rem(y + v, 4), me).start()
    ra[me] = jnp.zeros((32, 256), bf16)
    part[...] = own[quarter(32), :]
    w = ra.at[pl.ds(0, 31)]
    remote(w, w, s_oa, r_oa, side).wait_recv()

    def add_a(t):
        part[...] += ((ra[4 * t].astype(f32) + ra[4 * t + 1].astype(f32))
                      + (ra[4 * t + 2].astype(f32) + ra[4 * t + 3].astype(f32)))

    each(0, 8, add_a)

    def both(f):
        @pl.when(owner)
        def _():
            f(rb.at[pl.ds(0, 7)])

        @pl.when(jnp.logical_not(owner))
        def _():
            f(rb)

    both(lambda v: remote(v, v, s_ob, r_ob, side).wait_recv())
    part[...] += (((rb[0].astype(f32) + rb[1].astype(f32)) + (rb[2].astype(f32) + rb[3].astype(f32)))
                  + ((rb[4].astype(f32) + rb[5].astype(f32)) + (rb[6].astype(f32) + rb[7].astype(f32))))

    for t in range(1, 4):
        remote(part, out.at[quarter(32)], s_o, r_o, (z, x, c, rem(y + t, 4))).start()
    out[quarter(32), :] = part[...]

    both(lambda v: remote(v, v, s_ob, r_ob, side).wait_send())
    remote(w, w, s_oa, r_oa, side).wait_send()
    w = pa.at[pl.ds(0, 7)]
    remote(w, w, s_a, r_a.at[0], side).wait_send()
    for k, (vy, vr) in enumerate(((igy, igot), (fcy, fcr), (fdy, fdr))):
        w = vy.at[pl.ds(0, 3)]
        remote(w, w, s_y.at[k], r_y.at[k], side).wait_send()
        w = vr.at[pl.ds(0, 7)]
        remote(w, w, s_r.at[k], r_r.at[k], side).wait_send()
    w = pa.at[0, pl.ds(0, 48)]
    n_b = 7

    def sent_b(t):
        remote(w, w, s_b, r_b.at[0], side).wait_send()

    each(0, n_b, sent_b)

    @pl.when(jnp.logical_not(owner))
    def _():
        sent_b(0)

    w = out.at[pl.ds(0, 96)]
    remote(w, w, s_o, r_o, side).wait_recv()
    remote(w, w, s_o, r_o, side).wait_send()


def per_device(density, positions, areas, near_pairs, near_counts, far_pairs, far_counts, far_right, far_left):
    near = near_pairs[0, 0].transpose(1, 2, 0).reshape(8, 64)
    far = far_pairs[0, 0].transpose(1, 2, 0).reshape(4, 64)
    ncnt = near_counts.reshape(1, 64)
    fcnt = far_counts.reshape(1, 64)
    left = far_left.reshape(64, 64, 256)
    right = far_right.reshape(64, 64, 256)
    vm = pl.BlockSpec(memory_space=pltpu.VMEM)
    sm = pl.BlockSpec(memory_space=pltpu.SMEM)
    hbm = pl.BlockSpec(memory_space=pl.ANY)
    V, D = pltpu.VMEM, pltpu.SemaphoreType.DMA
    out = pl.pallas_call(
        kernel,
        out_shape=jax.ShapeDtypeStruct((128, 256), f32),
        in_specs=[vm] * 6 + [sm] * 2 + [hbm] * 2,
        out_specs=vm,
        scratch_shapes=[
            V((64, 64, 256), bf16), V((64, 64, 256), bf16), V((192, 256), bf16), V((8, 192, 256), bf16),
            V((2, 192, 256), bf16), V((8, 128), i32), V((8, 128), i32), V((4, 8, 128), i32), V((8, 4, 8, 128), i32),
            V((8, 128), i32), pltpu.SMEM((8, 128), i32), V((2, 128, 128), f32), V((32, KF, 256), bf16),
            V((32, 256, KF), bf16), V((32, 8, 256), f32), V((32, 8, 256), f32),
            V((16, 256, 256), bf16), V((16, 256, 256), bf16), V((256, 256), f32), V((256, 256), f32), V((256, 256), f32), V((128, 256), f32),
            V((4, 8, 32, 256), bf16), V((4, 8, 32, 256), bf16), V((8, 4, 32, 256), bf16),
            V((4, 8, 32, 256), bf16), V((4, 8, 32, 256), bf16), V((8, 4, 32, 256), bf16),
            V((8, 128, 256), bf16), V((2, 128, 256), bf16), V((32, 32, 256), bf16), V((8, 32, 256), bf16),
            V((32, 256), f32),
            D((5,)), D, D((8,)), D, D((2,)), D((3,)), D((3,)), D((3,)), D((3,)), D, D, D, D, D, D,
        ],
        compiler_params=pltpu.CompilerParams(collective_id=1, has_side_effects=True,
                                             vmem_limit_bytes=56 * 1024 * 1024),
    )(near, ncnt, far, density.reshape(128, 256), positions.transpose(1, 0, 2).reshape(48, 256), areas,
      far, fcnt, left, right)
    return out.reshape(16, 8, 256)


def solution(mesh):
    grid = Mesh(mesh.devices.reshape(8, 4, 2, 4), ("z", "x", "c", "y"))
    d = ("z", "x", "c")
    return jax.shard_map(
        per_device,
        mesh=grid,
        in_specs=(
            P(d, None, None),
            P(d, None, None),
            P(d, None),
            P(d, "y", None, None, None),
            P(d, "y", None),
            P(d, "y", None, None, None),
            P(d, "y", None),
            P(d, "y", None, None, None, None),
            P(d, "y", None, None, None, None),
        ),
        out_specs=P(d, None, None),
        check_vma=False,
    )
```
